32 devices in a mesh: groups: 2 (over y), tensor: 4 (over z), dp: 4 (over x, core).
Axes of the slice: x: 2, y: 2, z: 4, core: 2. Of those that a mesh axis runs over, the one named last changes fastest.
Arguments:
- residual: bfloat16 [16, 128, 8192], P(('groups', 'dp'), 'tensor'), parts along dimension 0, may hold values from -120 to 120
- norm_gain: bfloat16 [8192], replicated, may hold values from 0.099609375 to 1.8984375
- scale_exp: int32 [16, 128, 64], P(('groups', 'dp'), 'tensor'), parts along dimension 0, may hold values from -10 to -5
- w_query: bfloat16 [8192, 8192], P(None, 'tensor'), may hold values from -0.0625 to 0.0625
- q_bias: bfloat16 [8192], P('tensor'), may hold values from -5.5 to 5.5
- w_kv: bfloat16 [2, 8192, 1024], P(None, None, 'tensor'), may hold values from -0.0625 to 0.0625
- kv_bias: bfloat16 [2, 1024], P(None, 'tensor'), may hold values from -4 to 4
- w_out: bfloat16 [8192, 8192], P('tensor'), may hold values from -0.25 to 0.25
- kv_cache: bfloat16 [16, 2, 3968, 1024], P(('groups', 'dp'), None, 'tensor'), parts along dimension 0, may hold values from -8 to 8
- offsets: int32 [16], P(('groups', 'dp')), parts along dimension 0, may hold values from 0 to 3968, as said below
Outputs:
- mixed: bfloat16 [16, 128, 8192], P(('groups', 'dp'), 'tensor'), parts along dimension 0
- new_kv: bfloat16 [16, 2, 128, 1024], P(('groups', 'dp'), None, 'tensor'), parts along dimension 0
The draws below stay inside these ranges and needn't reach their ends.
There are 2 independent parts, one for each index of `groups`. The reference program is written for one: setup_inputs(seed, part) draws one part's arguments, and reference() takes and returns one part's arrays. A program takes and returns all parts, laid end to end along the dimension named above; an argument that names none is the same for every part. Nothing has to cross between parts.
Inputs may be any that keep to these rules, and one draw needn't show every extreme that they name: Each offset is a multiple of 128; sequence s has its prefix in cache slots 0 to offsets[s] - 1 and its span at positions offsets[s] onward. Some sequence of every part has offset 3968, and some has offset 0.
All inputs are finite; a program needn't handle non-finite values.
Results may differ from the reference program's by a relative error of at most 0.01115.
Values may be sent and summed in bfloat16 or wider, within the bound.
No kernel may reach another device: no remote copies, remote signals or barrier semaphores. Data moves between devices by JAX's collectives and lax.ppermute only.
A program may use at most 256 MiB of HBM per device.

```python
import math
import jax
import jax.numpy as jnp
from jax import lax

D = 8192
HEADS = 64
KVH = 8
HD = 128
SPAN = 128
CACHE = 3968
SEQS = 8
BLOCKS = 64


def block_levels(key):
    level_key, plant_key = jax.random.split(jax.random.fold_in(key, 101), 2)
    levels = jax.random.randint(level_key, (SEQS, SPAN, BLOCKS), 0, 5)
    planted = (jax.random.randint(plant_key, (SEQS, SPAN, BLOCKS), 0, 16) == 0).astype(jnp.int32)
    return (levels, planted)


def draw_residual(key, part):
    levels, planted = block_levels(key)
    key = jax.random.fold_in(key, 11)
    first_key = jax.random.fold_in(key, 0)
    third_key = jax.random.fold_in(key, 2)
    row_scale = jnp.exp(jax.random.uniform(first_key, (SEQS, SPAN, 1), minval=0.0, maxval=math.log(10.0)))
    level_scale = jnp.repeat(jnp.exp2(levels.astype(jnp.float32)), 128, axis=-1)
    base_draw = jnp.clip(jax.random.normal(third_key, (SEQS, SPAN, D)), -4.0, 4.0)
    values = base_draw * row_scale * level_scale * 0.15
    return values.astype(jnp.bfloat16)


def draw_scale_exp(key, part):
    levels, planted = block_levels(key)
    return (levels - 9 - planted).astype(jnp.int32)


def draw_q_bias(key, part):
    key = jax.random.fold_in(key, 12)
    third_key = jax.random.fold_in(key, 2)
    values = jnp.clip(jax.random.normal(third_key, (HEADS, HD)), -4.0, 4.0)
    return values.reshape(HEADS * HD).astype(jnp.bfloat16)


def draw_kv_cache(key, part):
    key = jax.random.fold_in(key, 13)
    first_key = jax.random.fold_in(key, 0)
    fourth_key = jax.random.fold_in(key, 3)
    width = KVH * HD
    key_draw = jnp.clip(1.2 * jax.random.normal(first_key, (SEQS, CACHE, width)), -8.0, 8.0)
    value_draw = jnp.clip(jax.random.normal(fourth_key, (SEQS, CACHE, width)), -4.0, 4.0)
    return jnp.stack([key_draw, value_draw], axis=1).astype(jnp.bfloat16)


def draw_offsets(key, part):
    key = jax.random.fold_in(key, 14)
    first_key, second_key = jax.random.split(key, 2)
    counts = jax.random.randint(first_key, (SEQS,), 0, CACHE // SPAN + 1) * SPAN
    top_index = jax.random.randint(second_key, (), 0, SEQS)
    empty_index = (top_index + 1) % SEQS
    seq_index = jnp.arange(SEQS)
    counts = jnp.where(seq_index == empty_index, 0, counts)
    return jnp.where(seq_index == top_index, CACHE, counts).astype(jnp.int32)


def block_scale(rng, dims, pieces, low, high):
    def one(axis_at, blocks):
        heights = jax.random.uniform(jax.random.fold_in(jax.random.fold_in(rng, 6), axis_at), (blocks,), jnp.float32, low / len(pieces), high / len(pieces))
        return jnp.repeat(jnp.exp(heights), dims[axis_at] // blocks).reshape((-1,) + (1,) * (len(dims) - axis_at - 1))

    gain = one(*pieces[0])
    for cut in pieces[1:]:
        gain = gain * one(*cut)
    return gain


def bell_draw(own_key, shape, scale, most, cuts=(), held_as=jnp.bfloat16):
    result = scale * jax.random.normal(own_key, shape, jnp.float32)
    if cuts:
        result = result * block_scale(own_key, shape, cuts, -0.22, 0.18)
    return jnp.clip(result, -most, most).astype(held_as)


def setup_inputs(seed: int = 0, part: int = 0) -> dict:
    key_list = jax.random.split(jax.random.key(seed), 11)
    own_keys = jax.random.split(jax.random.fold_in(key_list[10], part), 11)
    return {
        "residual": draw_residual(jax.random.fold_in(jax.random.fold_in(key_list[10], part), 71), part),
        "norm_gain": jnp.clip(1.0 + 0.18 * jax.random.normal(key_list[1], (D,), jnp.float32), 0.099609375, 1.8984375).astype(jnp.bfloat16),
        "scale_exp": draw_scale_exp(jax.random.fold_in(jax.random.fold_in(key_list[10], part), 71), part),
        "w_query": bell_draw(key_list[3], (D, HEADS * HD), D ** -0.5, 0.0625, ((1, 4),)),
        "q_bias": draw_q_bias(jax.random.fold_in(key_list[10], 71), part),
        "w_kv": bell_draw(key_list[5], (2, D, KVH * HD), D ** -0.5, 0.0625, ((2, 4),)),
        "kv_bias": bell_draw(key_list[6], (2, KVH * HD), 1.0, 4.0, ((1, 4),)),
        "w_out": bell_draw(key_list[7], (HEADS * HD, D), (HEADS * HD // 16) ** -0.5, 0.25, ((0, 4),)),
        "kv_cache": draw_kv_cache(jax.random.fold_in(jax.random.fold_in(key_list[10], part), 71), part),
        "offsets": draw_offsets(jax.random.fold_in(jax.random.fold_in(key_list[10], part), 71), part),
    }


EPSILON = 1e-06
CLIP_LIMIT = 448.0
MASKED_SCORE = -1e+30
NEVER_SEEN = 1 << 30

def encode_decode(residual, norm_gain, scale_exp):
    values = residual.astype(jnp.float32)
    mean_square = lax.optimization_barrier(jnp.mean(values * values, axis=-1, keepdims=True))
    normed = values * lax.rsqrt(mean_square + EPSILON) * norm_gain.astype(jnp.float32)
    full_shape = normed.shape
    blocks = normed.reshape(full_shape[:-1] + (full_shape[-1] // 128, 128))
    factor = jnp.exp2(scale_exp.astype(jnp.float32))[..., None]
    encoded = jnp.clip(blocks / factor, -CLIP_LIMIT, CLIP_LIMIT).astype(jnp.bfloat16)
    decoded = (encoded.astype(jnp.float32) * factor).astype(jnp.bfloat16)
    return decoded.reshape(full_shape)

def one_sequence(inputs):
    seq_queries, seq_cache, seq_new, prefix_len = inputs
    key_rows = jnp.concatenate([seq_cache[0], seq_new[0]], axis=0).reshape(CACHE + SPAN, KVH, HD)
    value_rows = jnp.concatenate([seq_cache[1], seq_new[1]], axis=0).reshape(CACHE + SPAN, KVH, HD)
    slot_index = jnp.arange(CACHE + SPAN, dtype=jnp.int32)
    key_rank = jnp.where(slot_index < CACHE, jnp.where(slot_index < prefix_len, -1, NEVER_SEEN), slot_index - CACHE)
    row_pos = jnp.arange(SPAN, dtype=jnp.int32)
    allowed = (key_rank[None, :] <= row_pos[:, None])[None, None]
    grouped = seq_queries.reshape(SPAN, KVH, HEADS // KVH, HD).astype(jnp.float32)
    scores = jnp.einsum('jagd,kad->agjk', grouped, key_rows.astype(jnp.float32), precision=lax.Precision.HIGHEST) / math.sqrt(HD)
    scores = jnp.where(allowed, scores, MASKED_SCORE)
    maxima = lax.optimization_barrier(jnp.max(scores, axis=-1, keepdims=True))
    weights = jnp.where(allowed, jnp.exp(scores - maxima), 0.0)
    totals = lax.optimization_barrier(jnp.sum(weights, axis=-1, keepdims=True))
    probs = lax.optimization_barrier(weights.astype(jnp.bfloat16))
    summed = jnp.einsum('agjk,kad->agjd', probs.astype(jnp.float32), value_rows.astype(jnp.float32), precision=lax.Precision.HIGHEST)
    attended = (summed / totals).astype(jnp.bfloat16)
    return attended.transpose(2, 0, 1, 3).reshape(SPAN, HEADS * HD)

def reference(residual, norm_gain, scale_exp, w_query, q_bias, w_kv, kv_bias, w_out, kv_cache, offsets):
    decoded = encode_decode(residual, norm_gain, scale_exp)
    flat_rows = decoded.reshape(SEQS * SPAN, D)
    queries = jnp.dot(flat_rows, w_query, preferred_element_type=jnp.float32) + q_bias.astype(jnp.float32)
    queries = queries.astype(jnp.bfloat16).reshape(SEQS, SPAN, HEADS * HD)
    fresh_kv = jnp.einsum('scd,kdq->skcq', decoded.astype(jnp.float32), w_kv.astype(jnp.float32), precision=lax.Precision.HIGHEST)
    new_kv = (fresh_kv + kv_bias.astype(jnp.float32)[None, :, None, :]).astype(jnp.bfloat16)
    attended = lax.map(one_sequence, (queries, kv_cache, new_kv, offsets))
    mixed = jnp.dot(attended.reshape(SEQS * SPAN, HEADS * HD), w_out, preferred_element_type=jnp.float32)
    mixed = mixed.astype(jnp.bfloat16).reshape(SEQS, SPAN, D)
    return (mixed, new_kv)
```

```python
import functools
import math

import jax
import jax.numpy as jnp
from jax import lax
from jax.experimental import pallas as pl
from jax.experimental.pallas import tpu as pltpu
from jax.sharding import PartitionSpec as P


HEADS = 64
KVH = 8
HD = 128


EPSILON = 1e-06
CLIP_LIMIT = 448.0
MASKED_SCORE = -1e30
NEVER_SEEN = 1 << 30


def encode_rows(residual, norm_gain, scale_exp):
    values = residual.astype(jnp.float32)
    mean_square = jnp.mean(values * values, axis=-1, keepdims=True)
    normed = values * lax.rsqrt(mean_square + EPSILON) * norm_gain.astype(jnp.float32)
    full_shape = normed.shape
    blocks = normed.reshape(full_shape[:-1] + (full_shape[-1] // 128, 128))
    factor = jnp.exp2(scale_exp.astype(jnp.float32))[..., None]
    encoded = jnp.clip(blocks / factor, -CLIP_LIMIT, CLIP_LIMIT).astype(jnp.bfloat16)
    return encoded.reshape(full_shape)


def decode_rows(encoded, scale_exp):
    full_shape = encoded.shape
    blocks = encoded.reshape(full_shape[:-1] + (full_shape[-1] // 128, 128)).astype(jnp.float32)
    factor = jnp.exp2(scale_exp.astype(jnp.float32))[..., None]
    return (blocks * factor).astype(jnp.bfloat16).reshape(full_shape)


def key_order(offsets, sources, cache_len, new_len):
    cache_pos = sources[:, None] * cache_len + jnp.arange(cache_len, dtype=jnp.int32)[None, :]
    cached = jnp.where(cache_pos[None] < offsets[:, None, None], -1, NEVER_SEEN).astype(jnp.int32)
    fresh_rank = sources[:, None] * new_len + jnp.arange(new_len, dtype=jnp.int32)[None, :]
    fresh_rank = jnp.broadcast_to(fresh_rank[None], (offsets.shape[0],) + fresh_rank.shape)
    return jnp.concatenate([cached, fresh_rank], axis=2).reshape(offsets.shape[0], -1)


def attend(grouped, key_rows, value_rows, key_rank):
    scores = jnp.einsum(
        "sjagd,skad->sagjk", grouped, key_rows, preferred_element_type=jnp.float32
    ) / math.sqrt(HD)
    row_pos = jnp.arange(grouped.shape[1], dtype=jnp.int32)
    allowed = (key_rank[:, None, :] <= row_pos[None, :, None])[:, None, None]
    scores = jnp.where(allowed, scores, MASKED_SCORE)
    maxima = jnp.max(scores, axis=-1)
    weights = jnp.where(allowed, jnp.exp(scores - maxima[..., None]), 0.0)
    totals = jnp.sum(weights, axis=-1)
    probs = weights.astype(jnp.bfloat16)
    summed = jnp.einsum("sagjk,skad->sagjd", probs, value_rows, preferred_element_type=jnp.float32)
    return (summed, maxima, totals)


def general_body(residual, norm_gain, scale_exp, w_query, q_bias, w_kv, kv_bias, w_out, kv_cache, offsets):
    encoded = encode_rows(residual, norm_gain, scale_exp)
    encoded_all, exponents = (
        lax.all_gather(encoded, "tensor", axis=1, tiled=True),
        lax.all_gather(scale_exp, "tensor", axis=1, tiled=True),
    )
    decoded = decode_rows(encoded_all, exponents)
    seq_count, span_len, model_width = decoded.shape
    queries = jnp.einsum("scd,dq->scq", decoded, w_query, preferred_element_type=jnp.float32)
    queries = (queries + q_bias.astype(jnp.float32)).astype(jnp.bfloat16)
    fresh_kv = jnp.einsum("scd,kdq->skcq", decoded, w_kv, preferred_element_type=jnp.float32)
    fresh_kv = (fresh_kv + kv_bias.astype(jnp.float32)[None, :, None, :]).astype(jnp.bfloat16)
    new_kv = lax.all_to_all(fresh_kv, "tensor", split_axis=2, concat_axis=3, tiled=True)
    cache_len = kv_cache.shape[2]
    new_len = new_kv.shape[2]
    local_kv = jnp.concatenate([kv_cache, new_kv], axis=2)
    key_count = local_kv.shape[2]
    heads_here = queries.shape[2] // HD
    group_size = HEADS // KVH
    repeat = max(1, group_size // heads_here)
    kv_here_count = max(1, heads_here // group_size)
    tensor_size = lax.axis_size("tensor")
    spread = jnp.broadcast_to(
        local_kv.reshape(seq_count, 2, key_count, KVH, 1, HD),
        (seq_count, 2, key_count, KVH, repeat, HD),
    )
    spread = spread.reshape(seq_count, 2, key_count, tensor_size, kv_here_count * HD)
    gathered = lax.all_to_all(spread, "tensor", split_axis=3, concat_axis=2, tiled=True)
    key_rows = gathered[:, 0].reshape(seq_count, -1, kv_here_count, HD)
    value_rows = gathered[:, 1].reshape(seq_count, -1, kv_here_count, HD)
    sources = jnp.arange(tensor_size, dtype=jnp.int32)
    key_rank = key_order(offsets, sources, cache_len, new_len)
    grouped = queries.reshape(seq_count, span_len, kv_here_count, heads_here // kv_here_count, HD)
    summed, maxima, totals = attend(grouped, key_rows, value_rows, key_rank)
    attended = (summed / totals[..., None]).astype(jnp.bfloat16)
    flipped = attended.transpose(3, 0, 1, 2, 4).reshape(span_len, seq_count, -1)
    summed_out = lax.psum_scatter(
        jnp.einsum("csq,qd->csd", flipped, w_out, preferred_element_type=jnp.float32).astype(
            jnp.bfloat16
        ),
        "tensor",
        scatter_dimension=0,
        tiled=True,
    ).astype(jnp.float32)
    mixed = summed_out.transpose(1, 0, 2).astype(jnp.bfloat16)
    return (mixed, new_kv)


MIB = 1 << 20
LOG2E_SCALE = math.log2(math.e) / math.sqrt(HD)
GROUP = HEADS // KVH
STAT = 128


def params(mib, n=0):
    if n:
        return pltpu.CompilerParams(vmem_limit_bytes=mib * MIB, dimension_semantics=("arbitrary",) * n)
    return pltpu.CompilerParams(vmem_limit_bytes=mib * MIB)


def whole(shape):
    return pl.BlockSpec(shape, lambda *_: (0,) * len(shape))


def encode_kernel(res_ref, gain_ref, exp_ref, *out_refs):
    for s, out_ref in enumerate(out_refs):
        values = res_ref[s].astype(jnp.float32)
        width = values.shape[-1]
        mean_square = jnp.sum(values * values, axis=-1, keepdims=True) * (1.0 / width)
        inv = lax.rsqrt(mean_square + EPSILON)
        exps = exp_ref[s]
        up = jnp.left_shift(jnp.int32(1), 16 + exps).astype(jnp.float32) * (1.0 / 65536.0)
        down = jnp.left_shift(jnp.int32(1), -exps).astype(jnp.float32)
        for b in range(width // 128):
            cols = slice(b * 128, (b + 1) * 128)
            normed = values[:, cols] * inv * gain_ref[:, cols].astype(jnp.float32)
            encoded = jnp.clip(normed * down[:, b : b + 1], -CLIP_LIMIT, CLIP_LIMIT).astype(jnp.bfloat16)
            out_ref[:, cols] = (encoded.astype(jnp.float32) * up[:, b : b + 1]).astype(jnp.bfloat16)


def encode_tokens(residual, norm_gain, scale_exp):
    seqs, rows, width = residual.shape
    return pl.pallas_call(
        encode_kernel,
        out_shape=[jax.ShapeDtypeStruct((rows, width), jnp.bfloat16)] * seqs,
        compiler_params=params(24),
        name="encode",
        cost_estimate=pl.CostEstimate(flops=8 * residual.size, bytes_accessed=4 * residual.size, transcendentals=0),
    )(residual, norm_gain.reshape(1, width), scale_exp)


def project_kernel(n_ways, q_tiles, pos_ref, *refs):
    own_ref, ways = refs[0], refs[1 : 1 + 2 * n_ways]
    wq_ref, qb_ref, wkv_ref, kvb_ref, q_ref, kv_ref, x_ref = refs[1 + 2 * n_ways :]
    step = pl.program_id(0)
    rows = own_ref.shape[0]
    z = pos_ref[0]

    @pl.when(step == 0)
    def _():
        def put(block, ref):
            x_ref[pl.ds(pl.multiple_of(block * rows, rows), rows), :] = ref[...]

        put(z, own_ref)
        for d in range(1, n_ways + 1):
            pl.when(z - d >= 0)(functools.partial(put, z - d, ways[2 * d - 2]))
            pl.when(z + d <= n_ways)(functools.partial(put, z + d, ways[2 * d - 1]))

    @pl.when(step < q_tiles)
    def _():
        acc = jnp.dot(x_ref[...], wq_ref[...], preferred_element_type=jnp.float32)
        q_ref[...] = (acc + qb_ref[...].astype(jnp.float32)).astype(jnp.bfloat16)

    @pl.when(step >= q_tiles)
    def _():
        acc = jnp.dot(x_ref[...], wkv_ref[0], preferred_element_type=jnp.float32)
        kv_ref[0] = (acc + kvb_ref[0].astype(jnp.float32)).astype(jnp.bfloat16)


def project(pos, own, ways, w_query, q_bias, w_kv, kv_bias, tile):
    rows, width = own.shape
    n_ways = len(ways) // 2
    span = rows * (n_ways + 1)
    q_cols, kv_cols = w_query.shape[1], w_kv.shape[2]
    q_tiles = q_cols // tile
    q_at = lambda i, pos: (0, jnp.minimum(i, q_tiles - 1))
    kv_at = lambda i, pos: (jnp.maximum(i - q_tiles, 0), 0, 0)
    return pl.pallas_call(
        functools.partial(project_kernel, n_ways, q_tiles),
        grid_spec=pltpu.PrefetchScalarGridSpec(
            num_scalar_prefetch=1,
            grid=(q_tiles + 2,),
            in_specs=[whole((rows, width))] * (1 + 2 * n_ways)
            + [
                pl.BlockSpec((width, tile), q_at),
                pl.BlockSpec((1, tile), q_at),
                pl.BlockSpec((1, width, kv_cols), kv_at),
                pl.BlockSpec((1, 1, kv_cols), kv_at),
            ],
            out_specs=[pl.BlockSpec((span, tile), q_at), pl.BlockSpec((1, span, kv_cols), kv_at)],
            scratch_shapes=[pltpu.VMEM((span, width), jnp.bfloat16)],
        ),
        out_shape=[
            jax.ShapeDtypeStruct((span, q_cols), jnp.bfloat16),
            jax.ShapeDtypeStruct((2, span, kv_cols), jnp.bfloat16),
        ],
        compiler_params=params(48, 1),
        name="project",
        cost_estimate=pl.CostEstimate(
            flops=2 * span * width * (q_cols + 2 * kv_cols),
            bytes_accessed=2 * width * (q_cols + 2 * kv_cols),
            transcendentals=0,
        ),
    )(pos, own, *ways, w_query, q_bias.reshape(1, q_cols), w_kv, kv_bias.reshape(2, 1, kv_cols))


def split2(value):
    high = value.astype(jnp.bfloat16)
    low = (value - high.astype(jnp.float32)).astype(jnp.bfloat16)
    return high, low


def score(q, k):
    dims = (((1,), (1,)), ((), ()))
    return lax.dot_general(q, k, dims, preferred_element_type=jnp.float32) * LOG2E_SCALE


def stack_heads(q_ref, first, count):
    return jnp.concatenate([q_ref[:, (first + i) * HD : (first + i + 1) * HD] for i in range(count)], axis=0)


def put_column(ref, head, column):
    lane = lax.broadcasted_iota(jnp.int32, ref.shape, 1)
    ref[...] = jnp.where(lane == head, column, ref[...])


def shift_of(largest):
    high, low = split2(largest)
    return high.astype(jnp.float32) + low.astype(jnp.float32)


def pack_stats(m, l, heads):
    pieces = [*split2(m[:, :heads]), *split2(l[:, :heads])]
    pad = STAT - 4 * heads
    if pad:
        pieces.append(jnp.zeros((m.shape[0], pad), jnp.bfloat16))
    return jnp.concatenate(pieces, axis=1)


def read_stats(stat, heads):
    stat = stat.astype(jnp.float32)
    m = stat[:, :heads] + stat[:, heads : 2 * heads]
    l = stat[:, 2 * heads : 3 * heads] + stat[:, 3 * heads : 4 * heads]
    return jnp.where(l > 0.0, m, MASKED_SCORE), l


PAIR = 2


def far_kernel(kv_here, info_ref, qu_ref, qd_ref, k_ref, v_ref, ou_ref, od_ref, m_ref, l_ref, q_ref):
    way, a = pl.program_id(0), pl.program_id(1)
    valid, count = info_ref[4 + way], info_ref[0]
    heads = kv_here * GROUP
    slots = k_ref.shape[2]
    rows = qu_ref.shape[0]
    cols = GROUP * HD

    @pl.when(a == 0)
    def _():
        m_ref[...] = jnp.full(m_ref.shape, MASKED_SCORE, jnp.float32)
        l_ref[...] = jnp.zeros(l_ref.shape, jnp.float32)

    def run(out_ref, w):
        live = jnp.logical_and(valid > 0, count > 0)
        for kv in range(kv_here):

            @pl.when(jnp.logical_and(a == kv, live))
            def _():
                keys, values = k_ref[0, 0], v_ref[0, 0]
                slot = lax.broadcasted_iota(jnp.int32, (1, slots), 1)
                bias = jnp.where(slot < count, 0.0, MASKED_SCORE)
                for g in range(0, GROUP, PAIR):
                    head = kv * GROUP + g
                    s = score(stack_heads(w, head, PAIR), keys) + bias
                    m = shift_of(jnp.max(s, axis=-1, keepdims=True))
                    p = jnp.exp2(s - m)
                    l = jnp.sum(p, axis=-1, keepdims=True)
                    o = jnp.dot(p.astype(jnp.bfloat16), values, preferred_element_type=jnp.float32)
                    for i in range(PAIR):
                        part = slice(i * rows, (i + 1) * rows)
                        put_column(m_ref, head + i, m[part])
                        put_column(l_ref, head + i, l[part])
                        out_ref[:, (head + i) * HD : (head + i + 1) * HD] = o[part].astype(jnp.bfloat16)

            @pl.when(jnp.logical_and(a == kv, jnp.logical_not(live)))
            def _():
                out_ref[:, kv * cols : (kv + 1) * cols] = jnp.zeros((rows, cols), jnp.bfloat16)

        @pl.when(a == kv_here - 1)
        def _():
            out_ref[:, kv_here * cols :] = pack_stats(m_ref[...], l_ref[...], heads)

    pl.when(way == 0)(lambda: run(ou_ref, qu_ref))
    pl.when(way == 1)(lambda: run(od_ref, qd_ref))


def attend_far(count, z, n_tensor, d, seq, q_up, q_down, kv_cache):
    rows, q_cols = q_up.shape
    slots = kv_cache.shape[2]
    kv_here = q_cols // (GROUP * HD)
    up_ok, down_ok = z - d >= 0, z + d < n_tensor
    info = jnp.stack(
        [
            count,
            jnp.int32(0),
            jnp.where(up_ok, z - d, z + d),
            jnp.where(down_ok, z + d, z - d),
            up_ok.astype(jnp.int32),
            down_ok.astype(jnp.int32),
        ]
    ).astype(jnp.int32)
    info = info.at[2:4].set(jnp.clip(info[2:4], 0, n_tensor - 1))
    head_at = lambda part: (lambda w, a, info: (seq, part, 0, info[2 + w] * kv_here + a))
    out = jax.ShapeDtypeStruct((rows, q_cols + STAT), jnp.bfloat16)
    return pl.pallas_call(
        functools.partial(far_kernel, kv_here),
        grid_spec=pltpu.PrefetchScalarGridSpec(
            num_scalar_prefetch=1,
            grid=(2, kv_here),
            in_specs=[
                whole((rows, q_cols)),
                whole((rows, q_cols)),
                pl.BlockSpec((1, 1, slots, HD), head_at(0)),
                pl.BlockSpec((1, 1, slots, HD), head_at(1)),
            ],
            out_specs=[whole((rows, q_cols + STAT))] * 2,
            scratch_shapes=[
                pltpu.VMEM((rows, 128), jnp.float32),
                pltpu.VMEM((rows, 128), jnp.float32),
                pltpu.VMEM((8, 128), jnp.bfloat16),
            ],
        ),
        out_shape=[out, out],
        compiler_params=params(40, 2),
        name="attend_far",
        cost_estimate=pl.CostEstimate(
            flops=8 * rows * q_cols * slots, bytes_accessed=8 * slots * HD * kv_here, transcendentals=rows * slots * 16
        ),
    )(info, q_up, q_down, kv_cache, kv_cache)


def near_kernel(kv_here, info_ref, q_in_ref, k_ref, v_ref, new_ref, o_ref, m_ref, l_ref):
    a = pl.program_id(0)
    count = info_ref[0]
    heads = kv_here * GROUP
    slots = k_ref.shape[2]
    rows = q_in_ref.shape[0]
    cols = GROUP * HD

    @pl.when(a == 0)
    def _():
        m_ref[...] = jnp.full(m_ref.shape, MASKED_SCORE, jnp.float32)
        l_ref[...] = jnp.zeros(l_ref.shape, jnp.float32)

    for kv in range(kv_here):

        @pl.when(a == kv)
        def _():
            keys, values = k_ref[0, 0], v_ref[0, 0]
            new_keys = new_ref[0, :, kv * HD : (kv + 1) * HD]
            new_values = new_ref[1, :, kv * HD : (kv + 1) * HD]
            slot = lax.broadcasted_iota(jnp.int32, (1, slots), 1)
            bias = jnp.where(slot < count, 0.0, MASKED_SCORE)
            shape = (PAIR * rows, rows)
            token = lax.broadcasted_iota(jnp.int32, shape, 0) % rows
            seen = lax.broadcasted_iota(jnp.int32, shape, 1) <= token
            for g in range(0, GROUP, PAIR):
                head = kv * GROUP + g
                q = stack_heads(q_in_ref, head, PAIR)
                s = score(q, keys) + bias
                t = jnp.where(seen, score(q, new_keys), MASKED_SCORE)
                m = jnp.maximum(jnp.max(s, axis=-1, keepdims=True), jnp.max(t, axis=-1, keepdims=True))
                m = shift_of(m)
                p, r = jnp.exp2(s - m), jnp.exp2(t - m)
                l = jnp.sum(p, axis=-1, keepdims=True) + jnp.sum(r, axis=-1, keepdims=True)
                o = jnp.dot(p.astype(jnp.bfloat16), values, preferred_element_type=jnp.float32)
                o += jnp.dot(r.astype(jnp.bfloat16), new_values, preferred_element_type=jnp.float32)
                for i in range(PAIR):
                    part = slice(i * rows, (i + 1) * rows)
                    put_column(m_ref, head + i, m[part])
                    put_column(l_ref, head + i, l[part])
                    o_ref[:, (head + i) * HD : (head + i + 1) * HD] = o[part].astype(jnp.bfloat16)

    @pl.when(a == kv_here - 1)
    def _():
        o_ref[:, kv_here * cols :] = pack_stats(m_ref[...], l_ref[...], heads)


def attend_near(count, z, seq, q, fresh, kv_cache):
    rows, q_cols = q.shape
    slots = kv_cache.shape[2]
    kv_here = q_cols // (GROUP * HD)
    info = jnp.stack([count, z]).astype(jnp.int32)
    head_at = lambda part: (lambda a, info: (seq, part, 0, info[1] * kv_here + a))
    return pl.pallas_call(
        functools.partial(near_kernel, kv_here),
        grid_spec=pltpu.PrefetchScalarGridSpec(
            num_scalar_prefetch=1,
            grid=(kv_here,),
            in_specs=[
                whole((rows, q_cols)),
                pl.BlockSpec((1, 1, slots, HD), head_at(0)),
                pl.BlockSpec((1, 1, slots, HD), head_at(1)),
                whole(fresh.shape),
            ],
            out_specs=whole((rows, q_cols + STAT)),
            scratch_shapes=[pltpu.VMEM((rows, 128), jnp.float32), pltpu.VMEM((rows, 128), jnp.float32)],
        ),
        out_shape=jax.ShapeDtypeStruct((rows, q_cols + STAT), jnp.bfloat16),
        compiler_params=params(40, 1),
        name="attend_near",
        cost_estimate=pl.CostEstimate(
            flops=4 * rows * q_cols * (slots + rows),
            bytes_accessed=4 * slots * HD * kv_here,
            transcendentals=rows * (slots + rows) * 8,
        ),
    )(info, q, kv_cache, kv_cache, fresh)


def join(parts, heads):
    stats = [read_stats(part[:, heads * HD :], heads) for part in parts]
    top = functools.reduce(jnp.maximum, [m for m, _ in stats])
    gains = [jnp.exp2(m - top) for m, _ in stats]
    total = functools.reduce(jnp.add, [g * l for g, (_, l) in zip(gains, stats)])
    return gains, top, total


def joined_head(parts, gains, h):
    cols = slice(h * HD, (h + 1) * HD)
    return functools.reduce(jnp.add, [p[:, cols].astype(jnp.float32) * g[:, h : h + 1] for p, g in zip(parts, gains)])


def join_kernel(heads, a_ref, b_ref, c_ref, d_ref, up_ref, down_ref):
    for parts, out_ref in (((a_ref, b_ref), up_ref), ((c_ref, d_ref), down_ref)):
        gains, top, total = join(parts, heads)
        top = shift_of(top)
        for h in range(heads):
            out_ref[:, h * HD : (h + 1) * HD] = joined_head(parts, gains, h).astype(jnp.bfloat16)
        out_ref[:, heads * HD :] = pack_stats(top, total, heads)


def join_two(a, b, c, d):
    rows, width = a.shape
    out = jax.ShapeDtypeStruct((rows, width), jnp.bfloat16)
    return pl.pallas_call(
        functools.partial(join_kernel, (width - STAT) // HD),
        out_shape=[out, out],
        compiler_params=params(24),
        name="join",
        cost_estimate=pl.CostEstimate(flops=8 * a.size, bytes_accessed=12 * a.size, transcendentals=0),
    )(a, b, c, d)


def out_kernel(heads, n_parts, *refs):
    parts, (w_ref, o_ref, x_ref) = refs[:n_parts], refs[n_parts:]

    @pl.when(pl.program_id(0) == 0)
    def _():
        gains, _, total = join(parts, heads)
        inv = 1.0 / total
        gains = [g * inv for g in gains]
        for h in range(heads):
            x_ref[:, h * HD : (h + 1) * HD] = joined_head(parts, gains, h).astype(jnp.bfloat16)

    o_ref[...] = jnp.dot(x_ref[...], w_ref[...], preferred_element_type=jnp.float32).astype(jnp.bfloat16)


def project_out(parts, w_out, tile):
    rows, width = parts[0].shape
    heads = (width - STAT) // HD
    depth, cols = w_out.shape
    return pl.pallas_call(
        functools.partial(out_kernel, heads, len(parts)),
        grid=(cols // tile,),
        in_specs=[whole((rows, width))] * len(parts) + [pl.BlockSpec((depth, tile), lambda i: (0, i))],
        out_specs=pl.BlockSpec((rows, tile), lambda i: (0, i)),
        scratch_shapes=[pltpu.VMEM((rows, depth), jnp.bfloat16)],
        out_shape=jax.ShapeDtypeStruct((rows, cols), jnp.bfloat16),
        compiler_params=params(40, 1),
        name="project_out",
        cost_estimate=pl.CostEstimate(
            flops=2 * rows * depth * cols, bytes_accessed=2 * depth * cols + 2 * rows * cols, transcendentals=0
        ),
    )(*parts, w_out)


def hop(value, n, reach, up):
    if up:
        pairs = [(i, i + 1) for i in range(reach - 1, n - 1)]
    else:
        pairs = [(i, i - 1) for i in range(n - reach, 0, -1)]
    return lax.ppermute(value, "tensor", pairs)


def home(value, n, distance, up):
    if up:
        pairs = [(i, i + 1) for i in range(0, n - distance)]
    else:
        pairs = [(i, i - 1) for i in range(n - 1, distance - 1, -1)]
    return lax.ppermute(value, "tensor", pairs)


def spread(own, n):
    ups, downs = [own], [own]
    for d in range(1, n):
        ups.append(hop(ups[-1], n, d, True))
        downs.append(hop(downs[-1], n, d, False))
    return ups, downs


def line_body(residual, norm_gain, scale_exp, w_query, q_bias, w_kv, kv_bias, w_out, kv_cache, offsets):
    n = lax.axis_size("tensor")
    z = lax.axis_index("tensor")
    seqs, rows, width = residual.shape
    slots = kv_cache.shape[2]
    counts = jnp.clip(offsets - z * slots, 0, slots)
    pos = z.reshape(1).astype(jnp.int32)
    owns = encode_tokens(residual, norm_gain, scale_exp)
    mixed, fresh_all = [], []
    for s in range(seqs):
        ups, downs = spread(owns[s], n)
        ways = [w for d in range(1, n) for w in (ups[d], downs[d])]
        queries, fresh = project(pos, owns[s], ways, w_query, q_bias, w_kv, kv_bias, w_kv.shape[2])
        fresh_all.append(fresh)
        q_ups, q_downs = spread(queries, n)
        near = attend_near(counts[s], z, s, queries, fresh, kv_cache)
        far = {}
        for d in range(1, n):
            far[d] = attend_far(counts[s], z, n, d, s, q_ups[d], q_downs[d], kv_cache)
        go_down, go_up = far[n - 1]
        for d in range(n - 1, 0, -1):
            got_down, got_up = home(go_down, n, d, False), home(go_up, n, d, True)
            if d > 1:
                go_down, go_up = join_two(got_down, far[d - 1][0], got_up, far[d - 1][1])
        partial = project_out([near, got_down, got_up], w_out, 512)
        mine = lambda d: lax.dynamic_slice_in_dim(partial, jnp.clip(z + d, 0, n - 1) * rows, rows, axis=0)
        add = lambda a, b: (a.astype(jnp.float32) + b.astype(jnp.float32)).astype(jnp.bfloat16)
        sum_up, sum_down = mine(n - 1), mine(1 - n)
        for d in range(n - 1, 0, -1):
            got_up, got_down = home(sum_up, n, d, True), home(sum_down, n, d, False)
            if d > 1:
                sum_up, sum_down = add(got_up, mine(d - 1)), add(got_down, mine(1 - d))
        total = mine(0).astype(jnp.float32) + got_up.astype(jnp.float32) + got_down.astype(jnp.float32)
        mixed.append(total.astype(jnp.bfloat16))
    new_kv = lax.all_to_all(jnp.stack(fresh_all), "tensor", split_axis=2, concat_axis=3, tiled=True)
    return jnp.stack(mixed), new_kv


def body(*args):
    heads_here = args[3].shape[1] // HD
    tensor_size = lax.axis_size("tensor")
    if heads_here % GROUP == 0 and 1 < tensor_size <= 8:
        return line_body(*args)
    return general_body(*args)


def solution(mesh):
    placed = (
        P(("groups", "dp"), "tensor", None),
        P(),
        P(("groups", "dp"), "tensor", None),
        P(None, "tensor"),
        P("tensor"),
        P(None, None, "tensor"),
        P(None, "tensor"),
        P("tensor", None),
        P(("groups", "dp"), None, "tensor", None),
        P(("groups", "dp")),
    )
    return jax.shard_map(
        body,
        mesh=mesh,
        in_specs=placed,
        out_specs=(P(("groups", "dp"), "tensor", None), P(("groups", "dp"), None, "tensor", None)),
        check_vma=False,
    )
```

```python
import functools
import math

import jax
import jax.numpy as jnp
from jax import lax
from jax.experimental import pallas as pl
from jax.experimental.pallas import tpu as pltpu
from jax.sharding import PartitionSpec as P


HEADS = 64
KVH = 8
HD = 128


EPSILON = 1e-06
CLIP_LIMIT = 448.0
MASKED_SCORE = -1e30
NEVER_SEEN = 1 << 30


def encode_rows(residual, norm_gain, scale_exp):
    values = residual.astype(jnp.float32)
    mean_square = jnp.mean(values * values, axis=-1, keepdims=True)
    normed = values * lax.rsqrt(mean_square + EPSILON) * norm_gain.astype(jnp.float32)
    full_shape = normed.shape
    blocks = normed.reshape(full_shape[:-1] + (full_shape[-1] // 128, 128))
    factor = jnp.exp2(scale_exp.astype(jnp.float32))[..., None]
    encoded = jnp.clip(blocks / factor, -CLIP_LIMIT, CLIP_LIMIT).astype(jnp.bfloat16)
    return encoded.reshape(full_shape)


def decode_rows(encoded, scale_exp):
    full_shape = encoded.shape
    blocks = encoded.reshape(full_shape[:-1] + (full_shape[-1] // 128, 128)).astype(jnp.float32)
    factor = jnp.exp2(scale_exp.astype(jnp.float32))[..., None]
    return (blocks * factor).astype(jnp.bfloat16).reshape(full_shape)


def key_order(offsets, sources, cache_len, new_len):
    cache_pos = sources[:, None] * cache_len + jnp.arange(cache_len, dtype=jnp.int32)[None, :]
    cached = jnp.where(cache_pos[None] < offsets[:, None, None], -1, NEVER_SEEN).astype(jnp.int32)
    fresh_rank = sources[:, None] * new_len + jnp.arange(new_len, dtype=jnp.int32)[None, :]
    fresh_rank = jnp.broadcast_to(fresh_rank[None], (offsets.shape[0],) + fresh_rank.shape)
    return jnp.concatenate([cached, fresh_rank], axis=2).reshape(offsets.shape[0], -1)


def attend(grouped, key_rows, value_rows, key_rank):
    scores = jnp.einsum(
        "sjagd,skad->sagjk", grouped, key_rows, preferred_element_type=jnp.float32
    ) / math.sqrt(HD)
    row_pos = jnp.arange(grouped.shape[1], dtype=jnp.int32)
    allowed = (key_rank[:, None, :] <= row_pos[None, :, None])[:, None, None]
    scores = jnp.where(allowed, scores, MASKED_SCORE)
    maxima = jnp.max(scores, axis=-1)
    weights = jnp.where(allowed, jnp.exp(scores - maxima[..., None]), 0.0)
    totals = jnp.sum(weights, axis=-1)
    probs = weights.astype(jnp.bfloat16)
    summed = jnp.einsum("sagjk,skad->sagjd", probs, value_rows, preferred_element_type=jnp.float32)
    return (summed, maxima, totals)


def general_body(residual, norm_gain, scale_exp, w_query, q_bias, w_kv, kv_bias, w_out, kv_cache, offsets):
    encoded = encode_rows(residual, norm_gain, scale_exp)
    encoded_all, exponents = (
        lax.all_gather(encoded, "tensor", axis=1, tiled=True),
        lax.all_gather(scale_exp, "tensor", axis=1, tiled=True),
    )
    decoded = decode_rows(encoded_all, exponents)
    seq_count, span_len, model_width = decoded.shape
    queries = jnp.einsum("scd,dq->scq", decoded, w_query, preferred_element_type=jnp.float32)
    queries = (queries + q_bias.astype(jnp.float32)).astype(jnp.bfloat16)
    fresh_kv = jnp.einsum("scd,kdq->skcq", decoded, w_kv, preferred_element_type=jnp.float32)
    fresh_kv = (fresh_kv + kv_bias.astype(jnp.float32)[None, :, None, :]).astype(jnp.bfloat16)
    new_kv = lax.all_to_all(fresh_kv, "tensor", split_axis=2, concat_axis=3, tiled=True)
    cache_len = kv_cache.shape[2]
    new_len = new_kv.shape[2]
    local_kv = jnp.concatenate([kv_cache, new_kv], axis=2)
    key_count = local_kv.shape[2]
    heads_here = queries.shape[2] // HD
    group_size = HEADS // KVH
    repeat = max(1, group_size // heads_here)
    kv_here_count = max(1, heads_here // group_size)
    tensor_size = lax.axis_size("tensor")
    spread = jnp.broadcast_to(
        local_kv.reshape(seq_count, 2, key_count, KVH, 1, HD),
        (seq_count, 2, key_count, KVH, repeat, HD),
    )
    spread = spread.reshape(seq_count, 2, key_count, tensor_size, kv_here_count * HD)
    gathered = lax.all_to_all(spread, "tensor", split_axis=3, concat_axis=2, tiled=True)
    key_rows = gathered[:, 0].reshape(seq_count, -1, kv_here_count, HD)
    value_rows = gathered[:, 1].reshape(seq_count, -1, kv_here_count, HD)
    sources = jnp.arange(tensor_size, dtype=jnp.int32)
    key_rank = key_order(offsets, sources, cache_len, new_len)
    grouped = queries.reshape(seq_count, span_len, kv_here_count, heads_here // kv_here_count, HD)
    summed, maxima, totals = attend(grouped, key_rows, value_rows, key_rank)
    attended = (summed / totals[..., None]).astype(jnp.bfloat16)
    flipped = attended.transpose(3, 0, 1, 2, 4).reshape(span_len, seq_count, -1)
    summed_out = lax.psum_scatter(
        jnp.einsum("csq,qd->csd", flipped, w_out, preferred_element_type=jnp.float32).astype(
            jnp.bfloat16
        ),
        "tensor",
        scatter_dimension=0,
        tiled=True,
    ).astype(jnp.float32)
    mixed = summed_out.transpose(1, 0, 2).astype(jnp.bfloat16)
    return (mixed, new_kv)


MIB = 1 << 20
LOG2E_SCALE = math.log2(math.e) / math.sqrt(HD)
GROUP = HEADS // KVH
STAT = 128


def params(mib, n=0):
    if n:
        return pltpu.CompilerParams(vmem_limit_bytes=mib * MIB, dimension_semantics=("arbitrary",) * n)
    return pltpu.CompilerParams(vmem_limit_bytes=mib * MIB)


def whole(shape):
    return pl.BlockSpec(shape, lambda *_: (0,) * len(shape))


def encode_kernel(res_ref, gain_ref, exp_ref, *out_refs):
    for s, out_ref in enumerate(out_refs):
        values = res_ref[s].astype(jnp.float32)
        width = values.shape[-1]
        mean_square = jnp.sum(values * values, axis=-1, keepdims=True) * (1.0 / width)
        inv = lax.rsqrt(mean_square + EPSILON)
        exps = exp_ref[s]
        up = jnp.left_shift(jnp.int32(1), 16 + exps).astype(jnp.float32) * (1.0 / 65536.0)
        down = jnp.left_shift(jnp.int32(1), -exps).astype(jnp.float32)
        for b in range(width // 128):
            cols = slice(b * 128, (b + 1) * 128)
            normed = values[:, cols] * inv * gain_ref[:, cols].astype(jnp.float32)
            encoded = jnp.clip(normed * down[:, b : b + 1], -CLIP_LIMIT, CLIP_LIMIT).astype(jnp.bfloat16)
            out_ref[:, cols] = (encoded.astype(jnp.float32) * up[:, b : b + 1]).astype(jnp.bfloat16)


def encode_tokens(residual, norm_gain, scale_exp):
    seqs, rows, width = residual.shape
    return pl.pallas_call(
        encode_kernel,
        out_shape=[jax.ShapeDtypeStruct((rows, width), jnp.bfloat16)] * seqs,
        compiler_params=params(24),
        name="encode",
        cost_estimate=pl.CostEstimate(flops=8 * residual.size, bytes_accessed=4 * residual.size, transcendentals=0),
    )(residual, norm_gain.reshape(1, width), scale_exp)


def project_kernel(n_ways, q_tiles, pos_ref, *refs):
    own_ref, ways = refs[0], refs[1 : 1 + 2 * n_ways]
    wq_ref, qb_ref, wkv_ref, kvb_ref, q_ref, kv_ref, x_ref = refs[1 + 2 * n_ways :]
    step = pl.program_id(0)
    rows = own_ref.shape[0]
    z = pos_ref[0]

    @pl.when(step == 0)
    def _():
        def put(block, ref):
            x_ref[pl.ds(pl.multiple_of(block * rows, rows), rows), :] = ref[...]

        put(z, own_ref)
        for d in range(1, n_ways + 1):
            pl.when(z - d >= 0)(functools.partial(put, z - d, ways[2 * d - 2]))
            pl.when(z + d <= n_ways)(functools.partial(put, z + d, ways[2 * d - 1]))

    @pl.when(step < q_tiles)
    def _():
        acc = jnp.dot(x_ref[...], wq_ref[...], preferred_element_type=jnp.float32)
        q_ref[...] = (acc + qb_ref[...].astype(jnp.float32)).astype(jnp.bfloat16)

    @pl.when(step >= q_tiles)
    def _():
        for c in range(2):
            acc = jnp.dot(x_ref[...], wkv_ref[c], preferred_element_type=jnp.float32)
            kv_ref[c] = (acc + kvb_ref[c].astype(jnp.float32)).astype(jnp.bfloat16)


def project(pos, own, ways, w_query, q_bias, w_kv, kv_bias, tile):
    rows, width = own.shape
    n_ways = len(ways) // 2
    span = rows * (n_ways + 1)
    q_cols, kv_cols = w_query.shape[1], w_kv.shape[2]
    q_tiles = q_cols // tile
    q_at = lambda i, pos: (0, jnp.minimum(i, q_tiles - 1))
    return pl.pallas_call(
        functools.partial(project_kernel, n_ways, q_tiles),
        grid_spec=pltpu.PrefetchScalarGridSpec(
            num_scalar_prefetch=1,
            grid=(q_tiles + 1,),
            in_specs=[whole((rows, width))] * (1 + 2 * n_ways)
            + [
                pl.BlockSpec((width, tile), q_at),
                pl.BlockSpec((1, tile), q_at),
                whole((2, width, kv_cols)),
                whole((2, 1, kv_cols)),
            ],
            out_specs=[pl.BlockSpec((span, tile), q_at), whole((2, span, kv_cols))],
            scratch_shapes=[pltpu.VMEM((span, width), jnp.bfloat16)],
        ),
        out_shape=[
            jax.ShapeDtypeStruct((span, q_cols), jnp.bfloat16),
            jax.ShapeDtypeStruct((2, span, kv_cols), jnp.bfloat16),
        ],
        compiler_params=params(54, 1),
        name="project",
        cost_estimate=pl.CostEstimate(
            flops=2 * span * width * (q_cols + 2 * kv_cols),
            bytes_accessed=2 * width * (q_cols + 2 * kv_cols),
            transcendentals=0,
        ),
    )(pos, own, *ways, w_query, q_bias.reshape(1, q_cols), w_kv, kv_bias.reshape(2, 1, kv_cols))


def split2(value):
    high = value.astype(jnp.bfloat16)
    low = (value - high.astype(jnp.float32)).astype(jnp.bfloat16)
    return high, low


def score(q, k):
    dims = (((1,), (1,)), ((), ()))
    return lax.dot_general(q, k, dims, preferred_element_type=jnp.float32) * LOG2E_SCALE


def stack_heads(q_ref, first, count):
    return jnp.concatenate([q_ref[:, (first + i) * HD : (first + i + 1) * HD] for i in range(count)], axis=0)


def put_column(ref, head, column):
    lane = lax.broadcasted_iota(jnp.int32, ref.shape, 1)
    ref[...] = jnp.where(lane == head, column, ref[...])


def shift_of(largest):
    high, low = split2(largest)
    return high.astype(jnp.float32) + low.astype(jnp.float32)


def pack_stats(m, l, heads):
    pieces = [*split2(m[:, :heads]), *split2(l[:, :heads])]
    pad = STAT - 4 * heads
    if pad:
        pieces.append(jnp.zeros((m.shape[0], pad), jnp.bfloat16))
    return jnp.concatenate(pieces, axis=1)


def read_stats(stat, heads):
    stat = stat.astype(jnp.float32)
    m = stat[:, :heads] + stat[:, heads : 2 * heads]
    l = stat[:, 2 * heads : 3 * heads] + stat[:, 3 * heads : 4 * heads]
    return jnp.where(l > 0.0, m, MASKED_SCORE), l


PAIR = 2


def far_kernel(kv_here, n_tensor, d, seq, info_ref, qu_ref, qd_ref, k_ref, v_ref, ou_ref, od_ref, m_ref, l_ref):
    way, a = pl.program_id(0), pl.program_id(1)
    z, count = info_ref[0], info_ref[1 + seq]
    valid = jnp.where(way == 0, z >= d, z + d < n_tensor)
    heads = kv_here * GROUP
    slots = k_ref.shape[2]
    rows = qu_ref.shape[0]
    cols = GROUP * HD

    @pl.when(a == 0)
    def _():
        m_ref[...] = jnp.full(m_ref.shape, MASKED_SCORE, jnp.float32)
        l_ref[...] = jnp.zeros(l_ref.shape, jnp.float32)

    def run(out_ref, w):
        live = jnp.logical_and(valid, count > 0)
        for kv in range(kv_here):

            @pl.when(jnp.logical_and(a == kv, live))
            def _():
                keys, values = k_ref[0, 0], v_ref[0, 0]
                slot = lax.broadcasted_iota(jnp.int32, (1, slots), 1)
                bias = jnp.where(slot < count, 0.0, MASKED_SCORE)
                for g in range(0, GROUP, PAIR):
                    head = kv * GROUP + g
                    s = score(stack_heads(w, head, PAIR), keys) + bias
                    m = shift_of(jnp.max(s, axis=-1, keepdims=True))
                    p = jnp.exp2(s - m)
                    l = jnp.sum(p, axis=-1, keepdims=True)
                    o = jnp.dot(p.astype(jnp.bfloat16), values, preferred_element_type=jnp.float32)
                    for i in range(PAIR):
                        part = slice(i * rows, (i + 1) * rows)
                        put_column(m_ref, head + i, m[part])
                        put_column(l_ref, head + i, l[part])
                        out_ref[:, (head + i) * HD : (head + i + 1) * HD] = o[part].astype(jnp.bfloat16)

            @pl.when(jnp.logical_and(a == kv, jnp.logical_not(live)))
            def _():
                out_ref[:, kv * cols : (kv + 1) * cols] = jnp.zeros((rows, cols), jnp.bfloat16)

        @pl.when(a == kv_here - 1)
        def _():
            out_ref[:, kv_here * cols :] = pack_stats(m_ref[...], l_ref[...], heads)

    pl.when(way == 0)(lambda: run(ou_ref, qu_ref))
    pl.when(way == 1)(lambda: run(od_ref, qd_ref))


def attend_far(info, n_tensor, d, seq, q_up, q_down, kv_cache):
    rows, q_cols = q_up.shape
    slots = kv_cache.shape[2]
    kv_here = q_cols // (GROUP * HD)

    def owner(w, z):
        up = jnp.where(z >= d, z - d, z + d)
        down = jnp.where(z + d < n_tensor, z + d, z - d)
        return jnp.clip(jnp.where(w == 0, up, down), 0, n_tensor - 1)

    head_at = lambda part: (lambda w, a, info: (seq, part, 0, owner(w, info[0]) * kv_here + a))
    out = jax.ShapeDtypeStruct((rows, q_cols + STAT), jnp.bfloat16)
    return pl.pallas_call(
        functools.partial(far_kernel, kv_here, n_tensor, d, seq),
        grid_spec=pltpu.PrefetchScalarGridSpec(
            num_scalar_prefetch=1,
            grid=(2, kv_here),
            in_specs=[
                whole((rows, q_cols)),
                whole((rows, q_cols)),
                pl.BlockSpec((1, 1, slots, HD), head_at(0)),
                pl.BlockSpec((1, 1, slots, HD), head_at(1)),
            ],
            out_specs=[whole((rows, q_cols + STAT))] * 2,
            scratch_shapes=[
                pltpu.VMEM((rows, 128), jnp.float32),
                pltpu.VMEM((rows, 128), jnp.float32),
            ],
        ),
        out_shape=[out, out],
        compiler_params=params(40, 2),
        name="attend_far",
        cost_estimate=pl.CostEstimate(
            flops=8 * rows * q_cols * slots, bytes_accessed=8 * slots * HD * kv_here, transcendentals=rows * slots * 16
        ),
    )(info, q_up, q_down, kv_cache, kv_cache)


def near_kernel(kv_here, seq, info_ref, q_in_ref, k_ref, v_ref, new_ref, o_ref, m_ref, l_ref):
    a = pl.program_id(0)
    count = info_ref[1 + seq]
    heads = kv_here * GROUP
    slots = k_ref.shape[2]
    rows = q_in_ref.shape[0]
    cols = GROUP * HD

    @pl.when(a == 0)
    def _():
        m_ref[...] = jnp.full(m_ref.shape, MASKED_SCORE, jnp.float32)
        l_ref[...] = jnp.zeros(l_ref.shape, jnp.float32)

    for kv in range(kv_here):

        @pl.when(a == kv)
        def _():
            keys, values = k_ref[0, 0], v_ref[0, 0]
            new_keys = new_ref[0, :, kv * HD : (kv + 1) * HD]
            new_values = new_ref[1, :, kv * HD : (kv + 1) * HD]
            slot = lax.broadcasted_iota(jnp.int32, (1, slots), 1)
            bias = jnp.where(slot < count, 0.0, MASKED_SCORE)
            shape = (PAIR * rows, rows)
            token = lax.broadcasted_iota(jnp.int32, shape, 0) % rows
            seen = lax.broadcasted_iota(jnp.int32, shape, 1) <= token
            for g in range(0, GROUP, PAIR):
                head = kv * GROUP + g
                q = stack_heads(q_in_ref, head, PAIR)
                s = score(q, keys) + bias
                t = jnp.where(seen, score(q, new_keys), MASKED_SCORE)
                m = jnp.maximum(jnp.max(s, axis=-1, keepdims=True), jnp.max(t, axis=-1, keepdims=True))
                m = shift_of(m)
                p, r = jnp.exp2(s - m), jnp.exp2(t - m)
                l = jnp.sum(p, axis=-1, keepdims=True) + jnp.sum(r, axis=-1, keepdims=True)
                o = jnp.dot(p.astype(jnp.bfloat16), values, preferred_element_type=jnp.float32)
                o += jnp.dot(r.astype(jnp.bfloat16), new_values, preferred_element_type=jnp.float32)
                for i in range(PAIR):
                    part = slice(i * rows, (i + 1) * rows)
                    put_column(m_ref, head + i, m[part])
                    put_column(l_ref, head + i, l[part])
                    o_ref[:, (head + i) * HD : (head + i + 1) * HD] = o[part].astype(jnp.bfloat16)

    @pl.when(a == kv_here - 1)
    def _():
        o_ref[:, kv_here * cols :] = pack_stats(m_ref[...], l_ref[...], heads)


def attend_near(info, seq, q, fresh, kv_cache):
    rows, q_cols = q.shape
    slots = kv_cache.shape[2]
    kv_here = q_cols // (GROUP * HD)
    head_at = lambda part: (lambda a, info: (seq, part, 0, info[0] * kv_here + a))
    return pl.pallas_call(
        functools.partial(near_kernel, kv_here, seq),
        grid_spec=pltpu.PrefetchScalarGridSpec(
            num_scalar_prefetch=1,
            grid=(kv_here,),
            in_specs=[
                whole((rows, q_cols)),
                pl.BlockSpec((1, 1, slots, HD), head_at(0)),
                pl.BlockSpec((1, 1, slots, HD), head_at(1)),
                whole(fresh.shape),
            ],
            out_specs=whole((rows, q_cols + STAT)),
            scratch_shapes=[pltpu.VMEM((rows, 128), jnp.float32), pltpu.VMEM((rows, 128), jnp.float32)],
        ),
        out_shape=jax.ShapeDtypeStruct((rows, q_cols + STAT), jnp.bfloat16),
        compiler_params=params(40, 1),
        name="attend_near",
        cost_estimate=pl.CostEstimate(
            flops=4 * rows * q_cols * (slots + rows),
            bytes_accessed=4 * slots * HD * kv_here,
            transcendentals=rows * (slots + rows) * 8,
        ),
    )(info, q, kv_cache, kv_cache, fresh)


def join(parts, heads):
    stats = [read_stats(part[:, heads * HD :], heads) for part in parts]
    top = functools.reduce(jnp.maximum, [m for m, _ in stats])
    gains = [jnp.exp2(m - top) for m, _ in stats]
    total = functools.reduce(jnp.add, [g * l for g, (_, l) in zip(gains, stats)])
    return gains, top, total


def joined_head(parts, gains, h):
    cols = slice(h * HD, (h + 1) * HD)
    return functools.reduce(jnp.add, [p[:, cols].astype(jnp.float32) * g[:, h : h + 1] for p, g in zip(parts, gains)])


def join_kernel(heads, a_ref, b_ref, c_ref, d_ref, up_ref, down_ref):
    for parts, out_ref in (((a_ref, b_ref), up_ref), ((c_ref, d_ref), down_ref)):
        gains, top, total = join(parts, heads)
        top = shift_of(top)
        for h in range(heads):
            out_ref[:, h * HD : (h + 1) * HD] = joined_head(parts, gains, h).astype(jnp.bfloat16)
        out_ref[:, heads * HD :] = pack_stats(top, total, heads)


def join_two(a, b, c, d):
    rows, width = a.shape
    out = jax.ShapeDtypeStruct((rows, width), jnp.bfloat16)
    return pl.pallas_call(
        functools.partial(join_kernel, (width - STAT) // HD),
        out_shape=[out, out],
        compiler_params=params(24),
        name="join",
        cost_estimate=pl.CostEstimate(flops=8 * a.size, bytes_accessed=12 * a.size, transcendentals=0),
    )(a, b, c, d)


def out_kernel(heads, n_parts, *refs):
    parts, (w_ref, o_ref, x_ref) = refs[:n_parts], refs[n_parts:]

    @pl.when(pl.program_id(0) == 0)
    def _():
        gains, _, total = join(parts, heads)
        inv = 1.0 / total
        gains = [g * inv for g in gains]
        for h in range(heads):
            x_ref[:, h * HD : (h + 1) * HD] = joined_head(parts, gains, h).astype(jnp.bfloat16)

    o_ref[...] = jnp.dot(x_ref[...], w_ref[...], preferred_element_type=jnp.float32).astype(jnp.bfloat16)


def project_out(parts, w_out, tile):
    rows, width = parts[0].shape
    heads = (width - STAT) // HD
    depth, cols = w_out.shape
    return pl.pallas_call(
        functools.partial(out_kernel, heads, len(parts)),
        grid=(cols // tile,),
        in_specs=[whole((rows, width))] * len(parts) + [pl.BlockSpec((depth, tile), lambda i: (0, i))],
        out_specs=pl.BlockSpec((rows, tile), lambda i: (0, i)),
        scratch_shapes=[pltpu.VMEM((rows, depth), jnp.bfloat16)],
        out_shape=jax.ShapeDtypeStruct((rows, cols), jnp.bfloat16),
        compiler_params=params(40, 1),
        name="project_out",
        cost_estimate=pl.CostEstimate(
            flops=2 * rows * depth * cols, bytes_accessed=2 * depth * cols + 2 * rows * cols, transcendentals=0
        ),
    )(*parts, w_out)


def hop(value, n, reach, up):
    if up:
        pairs = [(i, i + 1) for i in range(reach - 1, n - 1)]
    else:
        pairs = [(i, i - 1) for i in range(n - reach, 0, -1)]
    return lax.ppermute(value, "tensor", pairs)


def home(value, n, distance, up):
    if up:
        pairs = [(i, i + 1) for i in range(0, n - distance)]
    else:
        pairs = [(i, i - 1) for i in range(n - 1, distance - 1, -1)]
    return lax.ppermute(value, "tensor", pairs)


def after(value, *earlier):
    return lax.optimization_barrier((value, earlier))[0]


def hop_both(values, n, d):
    return hop(values[0], n, d, True), hop(values[1], n, d, False)


def home_both(values, n, d):
    return home(values[0], n, d, False), home(values[1], n, d, True)


def line_body(residual, norm_gain, scale_exp, w_query, q_bias, w_kv, kv_bias, w_out, kv_cache, offsets):
    n = lax.axis_size("tensor")
    z = lax.axis_index("tensor")
    seqs, rows, width = residual.shape
    slots = kv_cache.shape[2]
    last = n - 1
    counts = jnp.clip(offsets - z * slots, 0, slots)
    info = jnp.concatenate([z.reshape(1), counts]).astype(jnp.int32)
    owns = encode_tokens(residual, norm_gain, scale_exp)

    def projected(s, xs, *earlier):
        ways = [w for d in range(1, n) for w in xs[d]]
        own = after(owns[s], *earlier) if earlier else owns[s]
        return project(info, own, ways, w_query, q_bias, w_kv, kv_bias, 2 * w_kv.shape[2])

    def far(s, d, got, *earlier):
        up = after(got[0], *earlier) if earlier else got[0]
        return attend_far(info, n, d, s, up, got[1], kv_cache)

    def joined(got, own):
        return join_two(got[0], own[0], got[1], own[1])

    def mine(partial, d):
        return lax.dynamic_slice_in_dim(partial, jnp.clip(z + d, 0, last) * rows, rows, axis=0)

    def add(*terms):
        return functools.reduce(jnp.add, [t.astype(jnp.float32) for t in terms]).astype(jnp.bfloat16)

    x0, x1 = {0: (owns[0], owns[0])}, {}
    for d in range(1, n):
        if d == last:
            x1[0] = (after(owns[1], x0[d - 1]),) * 2
            x1[1] = hop_both(x1[0], n, 1)
        x0[d] = hop_both(x0[d - 1], n, d)
    q0, fresh0 = projected(0, x0, x1[1])
    for d in range(2, n):
        x1[d] = hop_both(x1[d - 1], n, d)
    g0, g1 = {0: (q0, q0)}, {}
    g0[1] = hop_both(g0[0], n, 1)
    near0 = attend_near(info, 0, q0, fresh0, kv_cache)
    g0[2] = hop_both(after(g0[1], near0), n, 2)
    q1, fresh1 = projected(1, x1, near0, g0[1])
    g1[0] = (q1, q1)
    for d in range(3, n):
        g0[d] = hop_both(after(g0[d - 1], q1), n, d)
    g1[1] = hop_both(g1[0], n, 1)
    f0, f1 = {}, {}
    f0[1] = far(0, 1, g0[1], q1)
    for d in range(2, n):
        f0[d] = far(0, d, g0[d], f0[d - 1])
        g1[d] = hop_both(after(g1[d - 1], f0[d - 1]), n, d)
    h0, h1 = {}, {}
    h0[last] = home_both(f0[last], n, last)
    near1 = attend_near(info, 1, after(q1, f0[last]), fresh1, kv_cache)
    f1[1] = far(1, 1, g1[1], near1)
    mark = f1[1]
    for d in range(last - 1, 0, -1):
        h0[d] = joined(after(h0[d + 1], mark), f0[d])
        mark = h0[d]
        h0[d] = home_both(h0[d], n, d)
        if d == last - 1:
            for e in range(2, n):
                f1[e] = far(1, e, g1[e], mark)
                mark = f1[e]
            h1[last] = home_both(f1[last], n, last)
    for d in range(last - 1, 0, -1):
        if d == 1:
            partial0 = project_out([near0, *after(h0[1], mark)], w_out, 2048)
            mark = partial0
        h1[d] = joined(after(h1[d + 1], mark), f1[d])
        mark = h1[d]
        h1[d] = home_both(h1[d], n, d)
    sums0 = home_both((mine(partial0, -last), mine(partial0, last)), n, last)
    partial1 = project_out([near1, *h1[1]], w_out, 2048)
    sums1 = home_both((mine(partial1, -last), mine(partial1, last)), n, last)
    for d in range(last - 1, 0, -1):
        sums0 = home_both((add(sums0[0], mine(partial0, -d)), add(sums0[1], mine(partial0, d))), n, d)
        sums1 = home_both((add(sums1[0], mine(partial1, -d)), add(sums1[1], mine(partial1, d))), n, d)
    mixed = [add(mine(partial0, 0), *sums0), add(mine(partial1, 0), *sums1)]
    fresh = after(jnp.stack([fresh0, fresh1]), partial1)
    new_kv = lax.all_to_all(fresh, "tensor", split_axis=2, concat_axis=3, tiled=True)
    return jnp.stack(mixed), new_kv


def body(*args):
    heads_here = args[3].shape[1] // HD
    tensor_size = lax.axis_size("tensor")
    if heads_here % GROUP == 0 and args[0].shape[0] == 2 and 2 < tensor_size <= 8:
        return line_body(*args)
    return general_body(*args)


def solution(mesh):
    placed = (
        P(("groups", "dp"), "tensor", None),
        P(),
        P(("groups", "dp"), "tensor", None),
        P(None, "tensor"),
        P("tensor"),
        P(None, None, "tensor"),
        P(None, "tensor"),
        P("tensor", None),
        P(("groups", "dp"), None, "tensor", None),
        P(("groups", "dp")),
    )
    return jax.shard_map(
        body,
        mesh=mesh,
        in_specs=placed,
        out_specs=(P(("groups", "dp"), "tensor", None), P(("groups", "dp"), None, "tensor", None)),
        check_vma=False,
    )
```

```python
import functools
import math

import jax
import jax.numpy as jnp
from jax import lax
from jax.experimental import pallas as pl
from jax.experimental.pallas import tpu as pltpu
from jax.sharding import PartitionSpec as P


HEADS = 64
KVH = 8
HD = 128


EPSILON = 1e-06
CLIP_LIMIT = 448.0
MASKED_SCORE = -1e30
NEVER_SEEN = 1 << 30


def encode_rows(residual, norm_gain, scale_exp):
    values = residual.astype(jnp.float32)
    mean_square = jnp.mean(values * values, axis=-1, keepdims=True)
    normed = values * lax.rsqrt(mean_square + EPSILON) * norm_gain.astype(jnp.float32)
    full_shape = normed.shape
    blocks = normed.reshape(full_shape[:-1] + (full_shape[-1] // 128, 128))
    factor = jnp.exp2(scale_exp.astype(jnp.float32))[..., None]
    encoded = jnp.clip(blocks / factor, -CLIP_LIMIT, CLIP_LIMIT).astype(jnp.bfloat16)
    return encoded.reshape(full_shape)


def decode_rows(encoded, scale_exp):
    full_shape = encoded.shape
    blocks = encoded.reshape(full_shape[:-1] + (full_shape[-1] // 128, 128)).astype(jnp.float32)
    factor = jnp.exp2(scale_exp.astype(jnp.float32))[..., None]
    return (blocks * factor).astype(jnp.bfloat16).reshape(full_shape)


def key_order(offsets, sources, cache_len, new_len):
    cache_pos = sources[:, None] * cache_len + jnp.arange(cache_len, dtype=jnp.int32)[None, :]
    cached = jnp.where(cache_pos[None] < offsets[:, None, None], -1, NEVER_SEEN).astype(jnp.int32)
    fresh_rank = sources[:, None] * new_len + jnp.arange(new_len, dtype=jnp.int32)[None, :]
    fresh_rank = jnp.broadcast_to(fresh_rank[None], (offsets.shape[0],) + fresh_rank.shape)
    return jnp.concatenate([cached, fresh_rank], axis=2).reshape(offsets.shape[0], -1)


def attend(grouped, key_rows, value_rows, key_rank):
    scores = jnp.einsum(
        "sjagd,skad->sagjk", grouped, key_rows, preferred_element_type=jnp.float32
    ) / math.sqrt(HD)
    row_pos = jnp.arange(grouped.shape[1], dtype=jnp.int32)
    allowed = (key_rank[:, None, :] <= row_pos[None, :, None])[:, None, None]
    scores = jnp.where(allowed, scores, MASKED_SCORE)
    maxima = jnp.max(scores, axis=-1)
    weights = jnp.where(allowed, jnp.exp(scores - maxima[..., None]), 0.0)
    totals = jnp.sum(weights, axis=-1)
    probs = weights.astype(jnp.bfloat16)
    summed = jnp.einsum("sagjk,skad->sagjd", probs, value_rows, preferred_element_type=jnp.float32)
    return (summed, maxima, totals)


def general_body(residual, norm_gain, scale_exp, w_query, q_bias, w_kv, kv_bias, w_out, kv_cache, offsets):
    encoded = encode_rows(residual, norm_gain, scale_exp)
    encoded_all, exponents = (
        lax.all_gather(encoded, "tensor", axis=1, tiled=True),
        lax.all_gather(scale_exp, "tensor", axis=1, tiled=True),
    )
    decoded = decode_rows(encoded_all, exponents)
    seq_count, span_len, model_width = decoded.shape
    queries = jnp.einsum("scd,dq->scq", decoded, w_query, preferred_element_type=jnp.float32)
    queries = (queries + q_bias.astype(jnp.float32)).astype(jnp.bfloat16)
    fresh_kv = jnp.einsum("scd,kdq->skcq", decoded, w_kv, preferred_element_type=jnp.float32)
    fresh_kv = (fresh_kv + kv_bias.astype(jnp.float32)[None, :, None, :]).astype(jnp.bfloat16)
    new_kv = lax.all_to_all(fresh_kv, "tensor", split_axis=2, concat_axis=3, tiled=True)
    cache_len = kv_cache.shape[2]
    new_len = new_kv.shape[2]
    local_kv = jnp.concatenate([kv_cache, new_kv], axis=2)
    key_count = local_kv.shape[2]
    heads_here = queries.shape[2] // HD
    group_size = HEADS // KVH
    repeat = max(1, group_size // heads_here)
    kv_here_count = max(1, heads_here // group_size)
    tensor_size = lax.axis_size("tensor")
    spread = jnp.broadcast_to(
        local_kv.reshape(seq_count, 2, key_count, KVH, 1, HD),
        (seq_count, 2, key_count, KVH, repeat, HD),
    )
    spread = spread.reshape(seq_count, 2, key_count, tensor_size, kv_here_count * HD)
    gathered = lax.all_to_all(spread, "tensor", split_axis=3, concat_axis=2, tiled=True)
    key_rows = gathered[:, 0].reshape(seq_count, -1, kv_here_count, HD)
    value_rows = gathered[:, 1].reshape(seq_count, -1, kv_here_count, HD)
    sources = jnp.arange(tensor_size, dtype=jnp.int32)
    key_rank = key_order(offsets, sources, cache_len, new_len)
    grouped = queries.reshape(seq_count, span_len, kv_here_count, heads_here // kv_here_count, HD)
    summed, maxima, totals = attend(grouped, key_rows, value_rows, key_rank)
    attended = (summed / totals[..., None]).astype(jnp.bfloat16)
    flipped = attended.transpose(3, 0, 1, 2, 4).reshape(span_len, seq_count, -1)
    summed_out = lax.psum_scatter(
        jnp.einsum("csq,qd->csd", flipped, w_out, preferred_element_type=jnp.float32).astype(
            jnp.bfloat16
        ),
        "tensor",
        scatter_dimension=0,
        tiled=True,
    ).astype(jnp.float32)
    mixed = summed_out.transpose(1, 0, 2).astype(jnp.bfloat16)
    return (mixed, new_kv)


MIB = 1 << 20
LOG2E_SCALE = math.log2(math.e) / math.sqrt(HD)
GROUP = HEADS // KVH
STAT = 128
LINE = 4


def two_away(z):
    return jnp.where(z >= 2, z - 2, z + 2)


def at_end(z):
    return jnp.logical_or(z == 0, z == LINE - 1)


def params(mib, n=0):
    if n:
        return pltpu.CompilerParams(vmem_limit_bytes=mib * MIB, dimension_semantics=("arbitrary",) * n)
    return pltpu.CompilerParams(vmem_limit_bytes=mib * MIB)


def whole(shape):
    return pl.BlockSpec(shape, lambda *_: (0,) * len(shape))


def encode_kernel(res_ref, gain_ref, exp_ref, *out_refs):
    for s, out_ref in enumerate(out_refs):
        values = res_ref[s].astype(jnp.float32)
        width = values.shape[-1]
        mean_square = jnp.sum(values * values, axis=-1, keepdims=True) * (1.0 / width)
        inv = lax.rsqrt(mean_square + EPSILON)
        exps = exp_ref[s]
        up = jnp.left_shift(jnp.int32(1), 16 + exps).astype(jnp.float32) * (1.0 / 65536.0)
        down = jnp.left_shift(jnp.int32(1), -exps).astype(jnp.float32)
        for b in range(width // 128):
            cols = slice(b * 128, (b + 1) * 128)
            normed = values[:, cols] * inv * gain_ref[:, cols].astype(jnp.float32)
            encoded = jnp.clip(normed * down[:, b : b + 1], -CLIP_LIMIT, CLIP_LIMIT).astype(jnp.bfloat16)
            out_ref[:, cols] = (encoded.astype(jnp.float32) * up[:, b : b + 1]).astype(jnp.bfloat16)


def encode_tokens(residual, norm_gain, scale_exp):
    seqs, rows, width = residual.shape
    return pl.pallas_call(
        encode_kernel,
        out_shape=[jax.ShapeDtypeStruct((rows, width), jnp.bfloat16)] * seqs,
        compiler_params=params(24),
        name="encode",
        cost_estimate=pl.CostEstimate(flops=8 * residual.size, bytes_accessed=4 * residual.size, transcendentals=0),
    )(residual, norm_gain.reshape(1, width), scale_exp)


def query_kernel(pos_ref, own_ref, up_ref, down_ref, two_ref, three_ref, w_ref, b_ref, q_ref, x_ref):
    rows = own_ref.shape[0]
    z = pos_ref[0]

    @pl.when(pl.program_id(0) == 0)
    def _():
        def put(block, ref):
            x_ref[pl.ds(pl.multiple_of(block * rows, rows), rows), :] = ref[...]

        put(z, own_ref)
        put(two_away(z), two_ref)
        pl.when(z > 0)(lambda: put(z - 1, up_ref))
        pl.when(z < LINE - 1)(lambda: put(z + 1, down_ref))
        pl.when(at_end(z))(lambda: put(LINE - 1 - z, three_ref))

    acc = jnp.dot(x_ref[...], w_ref[...], preferred_element_type=jnp.float32)
    q_ref[...] = (acc + b_ref[...].astype(jnp.float32)).astype(jnp.bfloat16)


def product_kernel(x_ref, w_ref, b_ref, o_ref):
    acc = jnp.dot(x_ref[...], w_ref[...], preferred_element_type=jnp.float32)
    o_ref[...] = (acc + b_ref[...].astype(jnp.float32)).astype(jnp.bfloat16)


def project_query(pos, own, others, w_query, q_bias, tile):
    rows, width = own.shape
    span = rows * LINE
    cols = w_query.shape[1]
    return pl.pallas_call(
        query_kernel,
        grid_spec=pltpu.PrefetchScalarGridSpec(
            num_scalar_prefetch=1,
            grid=(cols // tile,),
            in_specs=[whole((rows, width))] * (1 + len(others))
            + [pl.BlockSpec((width, tile), lambda i, pos: (0, i)), pl.BlockSpec((1, tile), lambda i, pos: (0, i))],
            out_specs=[pl.BlockSpec((span, tile), lambda i, pos: (0, i)), whole((span, width))],
        ),
        out_shape=[jax.ShapeDtypeStruct((span, cols), jnp.bfloat16), jax.ShapeDtypeStruct((span, width), jnp.bfloat16)],
        compiler_params=params(48, 1),
        name="project_query",
        cost_estimate=pl.CostEstimate(flops=2 * span * width * cols, bytes_accessed=2 * width * cols, transcendentals=0),
    )(pos, own, *others, w_query, q_bias.reshape(1, cols))


def project_fresh(features, w_kv, kv_bias):
    span, width = features.shape
    cols = w_kv.shape[2]
    spec = lambda shape: pl.BlockSpec((None,) + shape, lambda i: (i, 0, 0))
    return pl.pallas_call(
        product_kernel,
        grid=(2,),
        in_specs=[whole((span, width)), spec((width, cols)), spec((1, cols))],
        out_specs=spec((span, cols)),
        out_shape=jax.ShapeDtypeStruct((2, span, cols), jnp.bfloat16),
        compiler_params=params(24, 1),
        name="project_fresh",
        cost_estimate=pl.CostEstimate(flops=4 * span * width * cols, bytes_accessed=4 * width * cols, transcendentals=0),
    )(features, w_kv, kv_bias.reshape(2, 1, cols))


def split2(value):
    high = value.astype(jnp.bfloat16)
    low = (value - high.astype(jnp.float32)).astype(jnp.bfloat16)
    return high, low


def score(q, k):
    dims = (((1,), (1,)), ((), ()))
    return lax.dot_general(q, k, dims, preferred_element_type=jnp.float32) * LOG2E_SCALE


def stack_heads(q_ref, first, count):
    return jnp.concatenate([q_ref[:, (first + i) * HD : (first + i + 1) * HD] for i in range(count)], axis=0)


def put_column(ref, head, column):
    lane = lax.broadcasted_iota(jnp.int32, ref.shape, 1)
    ref[...] = jnp.where(lane == head, column, ref[...])


def shift_of(largest):
    high, low = split2(largest)
    return high.astype(jnp.float32) + low.astype(jnp.float32)


def pack_stats(m, l, heads):
    pieces = [*split2(m[:, :heads]), *split2(l[:, :heads])]
    pad = STAT - 4 * heads
    if pad:
        pieces.append(jnp.zeros((m.shape[0], pad), jnp.bfloat16))
    return jnp.concatenate(pieces, axis=1)


def read_stats(stat, heads):
    stat = stat.astype(jnp.float32)
    m = stat[:, :heads] + stat[:, heads : 2 * heads]
    l = stat[:, 2 * heads : 3 * heads] + stat[:, 3 * heads : 4 * heads]
    return jnp.where(l > 0.0, m, MASKED_SCORE), l


PAIR = 2


def owner_of(kind, z):
    if kind == "up":
        return jnp.maximum(z - 1, 0), z > 0
    if kind == "down":
        return jnp.minimum(z + 1, LINE - 1), z < LINE - 1
    if kind == "two":
        return two_away(z), z >= 0
    return jnp.where(at_end(z), LINE - 1 - z, z), at_end(z)


def far_kernel(kv_here, seq, kinds, info_ref, *refs):
    n_q = len(kinds)
    q_refs, (k_ref, v_ref), out_refs = refs[:n_q], refs[n_q : n_q + 2], refs[n_q + 2 : 2 * n_q + 2]
    m_ref, l_ref = refs[2 * n_q + 2 :]
    way, a = pl.program_id(0), pl.program_id(1)
    z, count = info_ref[0], info_ref[1 + seq]
    heads = kv_here * GROUP
    slots = k_ref.shape[2]
    rows = q_refs[0].shape[0]
    cols = GROUP * HD

    @pl.when(a == 0)
    def _():
        m_ref[...] = jnp.full(m_ref.shape, MASKED_SCORE, jnp.float32)
        l_ref[...] = jnp.zeros(l_ref.shape, jnp.float32)

    def run(q_ref, out_ref, valid):
        live = jnp.logical_and(valid, count > 0)
        for kv in range(kv_here):

            @pl.when(jnp.logical_and(a == kv, live))
            def _():
                keys, values = k_ref[0, 0], v_ref[0, 0]
                slot = lax.broadcasted_iota(jnp.int32, (1, slots), 1)
                bias = jnp.where(slot < count, 0.0, MASKED_SCORE)
                first = score(stack_heads(q_ref, kv * GROUP, PAIR), keys)
                got = []
                for g in range(0, GROUP, PAIR):
                    head = kv * GROUP + g
                    s = first + bias
                    if g + PAIR < GROUP:
                        first = score(stack_heads(q_ref, head + PAIR, PAIR), keys)
                    m = shift_of(jnp.max(s, axis=-1, keepdims=True))
                    p = jnp.exp2(s - m)
                    l = jnp.sum(p, axis=-1, keepdims=True)
                    o = jnp.dot(p.astype(jnp.bfloat16), values, preferred_element_type=jnp.float32)
                    got.append((head, m, l))
                    for i in range(PAIR):
                        part = slice(i * rows, (i + 1) * rows)
                        out_ref[:, (head + i) * HD : (head + i + 1) * HD] = o[part].astype(jnp.bfloat16)
                for head, m, l in got:
                    for i in range(PAIR):
                        part = slice(i * rows, (i + 1) * rows)
                        put_column(m_ref, head + i, m[part])
                        put_column(l_ref, head + i, l[part])

            @pl.when(jnp.logical_and(a == kv, jnp.logical_not(live)))
            def _():
                out_ref[:, kv * cols : (kv + 1) * cols] = jnp.zeros((rows, cols), jnp.bfloat16)

        @pl.when(a == kv_here - 1)
        def _():
            out_ref[:, kv_here * cols :] = pack_stats(m_ref[...], l_ref[...], heads)

    for w, kind in enumerate(kinds):
        pl.when(way == w)(functools.partial(run, q_refs[w], out_refs[w], owner_of(kind, z)[1]))


def attend_far(info, seq, kinds, queries, kv_cache):
    rows, q_cols = queries[0].shape
    slots = kv_cache.shape[2]
    kv_here = q_cols // (GROUP * HD)

    def owner(w, z):
        places = [owner_of(kind, z)[0] for kind in kinds]
        return functools.reduce(lambda rest, i: jnp.where(w == i, places[i], rest), range(len(kinds)), places[0])

    head_at = lambda part: (lambda w, a, info: (seq, part, 0, owner(w, info[0]) * kv_here + a))
    out = jax.ShapeDtypeStruct((rows, q_cols + STAT), jnp.bfloat16)
    return pl.pallas_call(
        functools.partial(far_kernel, kv_here, seq, kinds),
        grid_spec=pltpu.PrefetchScalarGridSpec(
            num_scalar_prefetch=1,
            grid=(len(kinds), kv_here),
            in_specs=[whole((rows, q_cols))] * len(kinds)
            + [pl.BlockSpec((1, 1, slots, HD), head_at(0)), pl.BlockSpec((1, 1, slots, HD), head_at(1))],
            out_specs=[whole((rows, q_cols + STAT))] * len(kinds),
            scratch_shapes=[pltpu.VMEM((rows, 128), jnp.float32), pltpu.VMEM((rows, 128), jnp.float32)],
        ),
        out_shape=[out] * len(kinds),
        compiler_params=params(40, 2),
        name="attend_far",
        cost_estimate=pl.CostEstimate(
            flops=4 * rows * q_cols * slots * len(kinds),
            bytes_accessed=4 * slots * HD * kv_here * len(kinds),
            transcendentals=rows * slots * 8 * len(kinds),
        ),
    )(info, *queries, kv_cache, kv_cache)


def near_kernel(kv_here, seq, info_ref, q_in_ref, k_ref, v_ref, new_ref, o_ref, m_ref, l_ref):
    a = pl.program_id(0)
    count = info_ref[1 + seq]
    heads = kv_here * GROUP
    slots = k_ref.shape[2]
    rows = q_in_ref.shape[0]
    cols = GROUP * HD

    @pl.when(a == 0)
    def _():
        m_ref[...] = jnp.full(m_ref.shape, MASKED_SCORE, jnp.float32)
        l_ref[...] = jnp.zeros(l_ref.shape, jnp.float32)

    for kv in range(kv_here):

        @pl.when(a == kv)
        def _():
            keys, values = k_ref[0, 0], v_ref[0, 0]
            new_keys = new_ref[0, :, kv * HD : (kv + 1) * HD]
            new_values = new_ref[1, :, kv * HD : (kv + 1) * HD]
            slot = lax.broadcasted_iota(jnp.int32, (1, slots), 1)
            bias = jnp.where(slot < count, 0.0, MASKED_SCORE)
            shape = (PAIR * rows, rows)
            token = lax.broadcasted_iota(jnp.int32, shape, 0) % rows
            seen = lax.broadcasted_iota(jnp.int32, shape, 1) <= token
            def scores(head):
                q = stack_heads(q_in_ref, head, PAIR)
                return score(q, keys), score(q, new_keys)

            first = scores(kv * GROUP)
            got = []
            for g in range(0, GROUP, PAIR):
                head = kv * GROUP + g
                s, t = first[0] + bias, jnp.where(seen, first[1], MASKED_SCORE)
                if g + PAIR < GROUP:
                    first = scores(head + PAIR)
                m = jnp.maximum(jnp.max(s, axis=-1, keepdims=True), jnp.max(t, axis=-1, keepdims=True))
                m = shift_of(m)
                p, r = jnp.exp2(s - m), jnp.exp2(t - m)
                l = jnp.sum(p, axis=-1, keepdims=True) + jnp.sum(r, axis=-1, keepdims=True)
                o = jnp.dot(p.astype(jnp.bfloat16), values, preferred_element_type=jnp.float32)
                o += jnp.dot(r.astype(jnp.bfloat16), new_values, preferred_element_type=jnp.float32)
                got.append((head, m, l))
                for i in range(PAIR):
                    part = slice(i * rows, (i + 1) * rows)
                    o_ref[:, (head + i) * HD : (head + i + 1) * HD] = o[part].astype(jnp.bfloat16)
            for head, m, l in got:
                for i in range(PAIR):
                    part = slice(i * rows, (i + 1) * rows)
                    put_column(m_ref, head + i, m[part])
                    put_column(l_ref, head + i, l[part])

    @pl.when(a == kv_here - 1)
    def _():
        o_ref[:, kv_here * cols :] = pack_stats(m_ref[...], l_ref[...], heads)


def attend_near(info, seq, q, fresh, kv_cache):
    rows, q_cols = q.shape
    slots = kv_cache.shape[2]
    kv_here = q_cols // (GROUP * HD)
    head_at = lambda part: (lambda a, info: (seq, part, 0, info[0] * kv_here + a))
    return pl.pallas_call(
        functools.partial(near_kernel, kv_here, seq),
        grid_spec=pltpu.PrefetchScalarGridSpec(
            num_scalar_prefetch=1,
            grid=(kv_here,),
            in_specs=[
                whole((rows, q_cols)),
                pl.BlockSpec((1, 1, slots, HD), head_at(0)),
                pl.BlockSpec((1, 1, slots, HD), head_at(1)),
                whole(fresh.shape),
            ],
            out_specs=whole((rows, q_cols + STAT)),
            scratch_shapes=[pltpu.VMEM((rows, 128), jnp.float32), pltpu.VMEM((rows, 128), jnp.float32)],
        ),
        out_shape=jax.ShapeDtypeStruct((rows, q_cols + STAT), jnp.bfloat16),
        compiler_params=params(40, 1),
        name="attend_near",
        cost_estimate=pl.CostEstimate(
            flops=4 * rows * q_cols * (slots + rows),
            bytes_accessed=4 * slots * HD * kv_here,
            transcendentals=rows * (slots + rows) * 8,
        ),
    )(info, q, kv_cache, kv_cache, fresh)


def join(parts, heads):
    stats = [read_stats(part[:, heads * HD :], heads) for part in parts]
    top = functools.reduce(jnp.maximum, [m for m, _ in stats])
    gains = [jnp.exp2(m - top) for m, _ in stats]
    total = functools.reduce(jnp.add, [g * l for g, (_, l) in zip(gains, stats)])
    return gains, top, total


def joined_head(parts, gains, h):
    cols = slice(h * HD, (h + 1) * HD)
    return functools.reduce(jnp.add, [p[:, cols].astype(jnp.float32) * g[:, h : h + 1] for p, g in zip(parts, gains)])


def join_kernel(heads, a_ref, b_ref, o_ref):
    parts = (a_ref, b_ref)
    gains, top, total = join(parts, heads)
    top = shift_of(top)
    for h in range(heads):
        o_ref[:, h * HD : (h + 1) * HD] = joined_head(parts, gains, h).astype(jnp.bfloat16)
    o_ref[:, heads * HD :] = pack_stats(top, total, heads)


def join_two(a, b):
    rows, width = a.shape
    return pl.pallas_call(
        functools.partial(join_kernel, (width - STAT) // HD),
        out_shape=jax.ShapeDtypeStruct((rows, width), jnp.bfloat16),
        compiler_params=params(24),
        name="join",
        cost_estimate=pl.CostEstimate(flops=8 * a.size, bytes_accessed=6 * a.size, transcendentals=0),
    )(a, b)


def join_pair_kernel(heads, info_ref, a_ref, b_ref, below_ref, above_ref, down_ref, up_ref):
    def run(from_below, from_above):
        for parts, out_ref in (((below_ref, from_above), down_ref), ((above_ref, from_below), up_ref)):
            gains, top, total = join(parts, heads)
            top = shift_of(top)
            for h in range(heads):
                out_ref[:, h * HD : (h + 1) * HD] = joined_head(parts, gains, h).astype(jnp.bfloat16)
            out_ref[:, heads * HD :] = pack_stats(top, total, heads)

    pl.when(info_ref[0] <= 1)(lambda: run(a_ref, b_ref))
    pl.when(info_ref[0] > 1)(lambda: run(b_ref, a_ref))


def join_pair(info, inward, middle, below, above):
    rows, width = below.shape
    out = jax.ShapeDtypeStruct((rows, width), jnp.bfloat16)
    return pl.pallas_call(
        functools.partial(join_pair_kernel, (width - STAT) // HD),
        grid_spec=pltpu.PrefetchScalarGridSpec(
            num_scalar_prefetch=1,
            grid=(1,),
            in_specs=[whole((rows, width))] * 4,
            out_specs=[whole((rows, width))] * 2,
        ),
        out_shape=[out, out],
        compiler_params=params(24, 1),
        name="join_pair",
        cost_estimate=pl.CostEstimate(flops=16 * below.size, bytes_accessed=12 * below.size, transcendentals=0),
    )(info, inward, middle, below, above)


def out_kernel(heads, n_parts, *refs):
    parts, (w_ref, o_ref, x_ref) = refs[:n_parts], refs[n_parts:]

    @pl.when(pl.program_id(0) == 0)
    def _():
        gains, _, total = join(parts, heads)
        inv = 1.0 / total
        gains = [g * inv for g in gains]
        for h in range(heads):
            x_ref[:, h * HD : (h + 1) * HD] = joined_head(parts, gains, h).astype(jnp.bfloat16)

    o_ref[...] = jnp.dot(x_ref[...], w_ref[...], preferred_element_type=jnp.float32).astype(jnp.bfloat16)


def project_out(parts, w_out, tile):
    rows, width = parts[0].shape
    heads = (width - STAT) // HD
    depth, cols = w_out.shape
    return pl.pallas_call(
        functools.partial(out_kernel, heads, len(parts)),
        grid=(cols // tile,),
        in_specs=[whole((rows, width))] * len(parts) + [pl.BlockSpec((depth, tile), lambda i: (0, i))],
        out_specs=pl.BlockSpec((rows, tile), lambda i: (0, i)),
        scratch_shapes=[pltpu.VMEM((rows, depth), jnp.bfloat16)],
        out_shape=jax.ShapeDtypeStruct((rows, cols), jnp.bfloat16),
        compiler_params=params(40, 1),
        name="project_out",
        cost_estimate=pl.CostEstimate(
            flops=2 * rows * depth * cols, bytes_accessed=2 * depth * cols + 2 * rows * cols, transcendentals=0
        ),
    )(*parts, w_out)


UP = [(0, 1), (1, 2), (2, 3)]
DOWN = [(1, 0), (2, 1), (3, 2)]
TWO = [(0, 2), (1, 3), (2, 0), (3, 1)]
MIDDLE = [(1, 2), (2, 1)]
OUTWARD = [(2, 3), (1, 0)]
INWARD = [(0, 1), (3, 2)]


def send(value, pairs):
    return lax.ppermute(value, "tensor", pairs)


def after(value, *earlier):
    return lax.optimization_barrier((value, earlier))[0]


def spread_near(value):
    return send(value, UP), send(value, DOWN), send(value, TWO)


def line_body(residual, norm_gain, scale_exp, w_query, q_bias, w_kv, kv_bias, w_out, kv_cache, offsets):
    z = lax.axis_index("tensor")
    rows = residual.shape[1]
    slots = kv_cache.shape[2]
    counts = jnp.clip(offsets - z * slots, 0, slots)
    info = jnp.concatenate([z.reshape(1), counts]).astype(jnp.int32)
    own0, own1 = encode_tokens(residual, norm_gain, scale_exp)
    tile = 2 * w_kv.shape[2]

    def far(seq, kinds, queries, *earlier):
        queries = list(queries)
        if earlier:
            queries[0] = after(queries[0], *earlier)
        return attend_far(info, seq, kinds, queries, kv_cache)

    def mine(partial, block):
        return lax.dynamic_slice_in_dim(partial, jnp.clip(block, 0, LINE - 1) * rows, rows, axis=0)

    def add(*terms):
        return functools.reduce(jnp.add, [t.astype(jnp.float32) for t in terms]).astype(jnp.bfloat16)

    def neighbours(value, *earlier):
        if earlier:
            value = after(value, *earlier)
        return [send(value, UP), send(value, DOWN)]

    def forward(up, down):
        up, down = send(up, UP[1:]), send(down, DOWN[:2])
        return jnp.where(z >= 2, up, down)

    x0 = neighbours(own0)
    x0.append(forward(*x0))
    x1 = neighbours(own1, x0[2])
    x0.append(send(x0[2], OUTWARD))
    q0, x0_all = project_query(info, after(own0, *x1), x0, w_query, q_bias, tile)
    x1.append(forward(*x1))
    x1.append(send(x1[2], OUTWARD))
    g0 = neighbours(q0)
    fresh0 = project_fresh(x0_all, w_kv, kv_bias)
    near0 = attend_near(info, 0, q0, fresh0, kv_cache)
    g0.append(forward(after(g0[0], near0), after(g0[1], near0)))
    q1, x1_all = project_query(info, after(own1, near0, g0[0]), x1, w_query, q_bias, tile)
    g0.append(send(after(g0[2], q1), OUTWARD))
    g1 = neighbours(q1)
    below0, above0 = far(0, ("up", "down"), g0[:2], q1)
    g1.append(forward(after(g1[0], below0), after(g1[1], below0)))
    (two0,) = far(0, ("two",), g0[2:3], below0)
    (three0,) = far(0, ("three",), g0[3:], two0)
    h0_three = send(three0, INWARD)
    g1.append(send(after(g1[2], two0), OUTWARD))
    fresh1 = project_fresh(after(x1_all, three0), w_kv, kv_bias)
    near1 = attend_near(info, 1, q1, fresh1, kv_cache)
    below1, above1 = far(1, ("up", "down"), g1[:2], near1)
    joined0 = join_two(after(h0_three, below1), two0)
    h0_inward, h0_middle = send(joined0, INWARD), send(joined0, MIDDLE)
    (two1,) = far(1, ("two",), g1[2:3], joined0)
    (three1,) = far(1, ("three",), g1[3:], two1)
    h1_three = send(three1, INWARD)
    down0, up0 = join_pair(info, after(h0_inward, three1), h0_middle, below0, above0)
    h0_down, h0_up = send(down0, DOWN), send(up0, UP)
    joined1 = join_two(after(h1_three, down0), two1)
    h1_inward, h1_middle = send(joined1, INWARD), send(joined1, MIDDLE)
    partial0 = project_out([near0, h0_up, after(h0_down, joined1)], w_out, 2048)
    down1, up1 = join_pair(info, after(h1_inward, partial0), h1_middle, below1, above1)
    h1_down, h1_up = send(down1, DOWN), send(up1, UP)

    def one_home(partial, inward):
        joined = add(inward, mine(partial, two_away(z)))
        return send(joined, INWARD), send(joined, MIDDLE)

    def two_home(partial, inward, middle):
        up = add(mine(partial, z + 1), jnp.where(z <= 1, inward, middle))
        down = add(mine(partial, z - 1), jnp.where(z <= 1, middle, inward))
        return send(up, UP), send(down, DOWN)

    s0 = send(mine(partial0, LINE - 1 - z), INWARD)
    partial1 = project_out([near1, h1_up, h1_down], w_out, 2048)
    s1 = send(mine(partial1, LINE - 1 - z), INWARD)
    s0, s1 = one_home(partial0, s0), one_home(partial1, s1)
    s0, s1 = two_home(partial0, *s0), two_home(partial1, *s1)
    mixed0 = add(mine(partial0, z), *s0)
    mixed1 = add(mine(partial1, z), *s1)
    fresh = after(jnp.stack([fresh0, fresh1]), partial1)
    new_kv = lax.all_to_all(fresh, "tensor", split_axis=2, concat_axis=3, tiled=True)
    return jnp.stack([mixed0, mixed1]), new_kv


def body(*args):
    heads_here = args[3].shape[1] // HD
    tensor_size = lax.axis_size("tensor")
    if heads_here % GROUP == 0 and args[0].shape[0] == 2 and tensor_size == LINE:
        return line_body(*args)
    return general_body(*args)


def solution(mesh):
    placed = (
        P(("groups", "dp"), "tensor", None),
        P(),
        P(("groups", "dp"), "tensor", None),
        P(None, "tensor"),
        P("tensor"),
        P(None, None, "tensor"),
        P(None, "tensor"),
        P("tensor", None),
        P(("groups", "dp"), None, "tensor", None),
        P(("groups", "dp")),
    )
    return jax.shard_map(
        body,
        mesh=mesh,
        in_specs=placed,
        out_specs=(P(("groups", "dp"), "tensor", None), P(("groups", "dp"), None, "tensor", None)),
        check_vma=False,
    )
```

```python
import functools
import math

import jax
import jax.numpy as jnp
from jax import lax
from jax.experimental import pallas as pl
from jax.experimental.pallas import tpu as pltpu
from jax.sharding import PartitionSpec as P


HEADS = 64
KVH = 8
HD = 128


EPSILON = 1e-06
CLIP_LIMIT = 448.0
MASKED_SCORE = -1e30
NEVER_SEEN = 1 << 30


def encode_rows(residual, norm_gain, scale_exp):
    values = residual.astype(jnp.float32)
    mean_square = jnp.mean(values * values, axis=-1, keepdims=True)
    normed = values * lax.rsqrt(mean_square + EPSILON) * norm_gain.astype(jnp.float32)
    full_shape = normed.shape
    blocks = normed.reshape(full_shape[:-1] + (full_shape[-1] // 128, 128))
    factor = jnp.exp2(scale_exp.astype(jnp.float32))[..., None]
    encoded = jnp.clip(blocks / factor, -CLIP_LIMIT, CLIP_LIMIT).astype(jnp.bfloat16)
    return encoded.reshape(full_shape)


def decode_rows(encoded, scale_exp):
    full_shape = encoded.shape
    blocks = encoded.reshape(full_shape[:-1] + (full_shape[-1] // 128, 128)).astype(jnp.float32)
    factor = jnp.exp2(scale_exp.astype(jnp.float32))[..., None]
    return (blocks * factor).astype(jnp.bfloat16).reshape(full_shape)


def key_order(offsets, sources, cache_len, new_len):
    cache_pos = sources[:, None] * cache_len + jnp.arange(cache_len, dtype=jnp.int32)[None, :]
    cached = jnp.where(cache_pos[None] < offsets[:, None, None], -1, NEVER_SEEN).astype(jnp.int32)
    fresh_rank = sources[:, None] * new_len + jnp.arange(new_len, dtype=jnp.int32)[None, :]
    fresh_rank = jnp.broadcast_to(fresh_rank[None], (offsets.shape[0],) + fresh_rank.shape)
    return jnp.concatenate([cached, fresh_rank], axis=2).reshape(offsets.shape[0], -1)


def attend(grouped, key_rows, value_rows, key_rank):
    scores = jnp.einsum(
        "sjagd,skad->sagjk", grouped, key_rows, preferred_element_type=jnp.float32
    ) / math.sqrt(HD)
    row_pos = jnp.arange(grouped.shape[1], dtype=jnp.int32)
    allowed = (key_rank[:, None, :] <= row_pos[None, :, None])[:, None, None]
    scores = jnp.where(allowed, scores, MASKED_SCORE)
    maxima = jnp.max(scores, axis=-1)
    weights = jnp.where(allowed, jnp.exp(scores - maxima[..., None]), 0.0)
    totals = jnp.sum(weights, axis=-1)
    probs = weights.astype(jnp.bfloat16)
    summed = jnp.einsum("sagjk,skad->sagjd", probs, value_rows, preferred_element_type=jnp.float32)
    return (summed, maxima, totals)


def general_body(residual, norm_gain, scale_exp, w_query, q_bias, w_kv, kv_bias, w_out, kv_cache, offsets):
    encoded = encode_rows(residual, norm_gain, scale_exp)
    encoded_all, exponents = (
        lax.all_gather(encoded, "tensor", axis=1, tiled=True),
        lax.all_gather(scale_exp, "tensor", axis=1, tiled=True),
    )
    decoded = decode_rows(encoded_all, exponents)
    seq_count, span_len, model_width = decoded.shape
    queries = jnp.einsum("scd,dq->scq", decoded, w_query, preferred_element_type=jnp.float32)
    queries = (queries + q_bias.astype(jnp.float32)).astype(jnp.bfloat16)
    fresh_kv = jnp.einsum("scd,kdq->skcq", decoded, w_kv, preferred_element_type=jnp.float32)
    fresh_kv = (fresh_kv + kv_bias.astype(jnp.float32)[None, :, None, :]).astype(jnp.bfloat16)
    new_kv = lax.all_to_all(fresh_kv, "tensor", split_axis=2, concat_axis=3, tiled=True)
    cache_len = kv_cache.shape[2]
    new_len = new_kv.shape[2]
    local_kv = jnp.concatenate([kv_cache, new_kv], axis=2)
    key_count = local_kv.shape[2]
    heads_here = queries.shape[2] // HD
    group_size = HEADS // KVH
    repeat = max(1, group_size // heads_here)
    kv_here_count = max(1, heads_here // group_size)
    tensor_size = lax.axis_size("tensor")
    spread = jnp.broadcast_to(
        local_kv.reshape(seq_count, 2, key_count, KVH, 1, HD),
        (seq_count, 2, key_count, KVH, repeat, HD),
    )
    spread = spread.reshape(seq_count, 2, key_count, tensor_size, kv_here_count * HD)
    gathered = lax.all_to_all(spread, "tensor", split_axis=3, concat_axis=2, tiled=True)
    key_rows = gathered[:, 0].reshape(seq_count, -1, kv_here_count, HD)
    value_rows = gathered[:, 1].reshape(seq_count, -1, kv_here_count, HD)
    sources = jnp.arange(tensor_size, dtype=jnp.int32)
    key_rank = key_order(offsets, sources, cache_len, new_len)
    grouped = queries.reshape(seq_count, span_len, kv_here_count, heads_here // kv_here_count, HD)
    summed, maxima, totals = attend(grouped, key_rows, value_rows, key_rank)
    attended = (summed / totals[..., None]).astype(jnp.bfloat16)
    flipped = attended.transpose(3, 0, 1, 2, 4).reshape(span_len, seq_count, -1)
    summed_out = lax.psum_scatter(
        jnp.einsum("csq,qd->csd", flipped, w_out, preferred_element_type=jnp.float32).astype(
            jnp.bfloat16
        ),
        "tensor",
        scatter_dimension=0,
        tiled=True,
    ).astype(jnp.float32)
    mixed = summed_out.transpose(1, 0, 2).astype(jnp.bfloat16)
    return (mixed, new_kv)


MIB = 1 << 20
LOG2E_SCALE = math.log2(math.e) / math.sqrt(HD)
GROUP = HEADS // KVH
STAT = 128
LINE = 4


def two_away(z):
    return jnp.where(z >= 2, z - 2, z + 2)


def at_end(z):
    return jnp.logical_or(z == 0, z == LINE - 1)


def params(mib, n=0):
    if n:
        return pltpu.CompilerParams(vmem_limit_bytes=mib * MIB, dimension_semantics=("arbitrary",) * n)
    return pltpu.CompilerParams(vmem_limit_bytes=mib * MIB)


def whole(shape):
    return pl.BlockSpec(shape, lambda *_: (0,) * len(shape))


def encode_kernel(res_ref, gain_ref, exp_ref, *out_refs):
    for s, out_ref in enumerate(out_refs):
        values = res_ref[s].astype(jnp.float32)
        width = values.shape[-1]
        mean_square = jnp.sum(values * values, axis=-1, keepdims=True) * (1.0 / width)
        inv = lax.rsqrt(mean_square + EPSILON)
        exps = exp_ref[s]
        up = jnp.left_shift(jnp.int32(1), 16 + exps).astype(jnp.float32) * (1.0 / 65536.0)
        down = jnp.left_shift(jnp.int32(1), -exps).astype(jnp.float32)
        for b in range(width // 128):
            cols = slice(b * 128, (b + 1) * 128)
            normed = values[:, cols] * inv * gain_ref[:, cols].astype(jnp.float32)
            encoded = jnp.clip(normed * down[:, b : b + 1], -CLIP_LIMIT, CLIP_LIMIT).astype(jnp.bfloat16)
            out_ref[:, cols] = (encoded.astype(jnp.float32) * up[:, b : b + 1]).astype(jnp.bfloat16)


def encode_tokens(residual, norm_gain, scale_exp):
    seqs, rows, width = residual.shape
    return pl.pallas_call(
        encode_kernel,
        out_shape=[jax.ShapeDtypeStruct((rows, width), jnp.bfloat16)] * seqs,
        compiler_params=params(24),
        name="encode",
        cost_estimate=pl.CostEstimate(flops=8 * residual.size, bytes_accessed=4 * residual.size, transcendentals=0),
    )(residual, norm_gain.reshape(1, width), scale_exp)


def query_kernel(pos_ref, own_ref, up_ref, down_ref, two_ref, three_ref, w_ref, b_ref, q_ref, x_ref):
    rows = own_ref.shape[0]
    z = pos_ref[0]

    @pl.when(pl.program_id(0) == 0)
    def _():
        def put(block, ref):
            x_ref[pl.ds(pl.multiple_of(block * rows, rows), rows), :] = ref[...]

        put(z, own_ref)
        put(two_away(z), two_ref)
        pl.when(z > 0)(lambda: put(z - 1, up_ref))
        pl.when(z < LINE - 1)(lambda: put(z + 1, down_ref))
        pl.when(at_end(z))(lambda: put(LINE - 1 - z, three_ref))

    acc = jnp.dot(x_ref[...], w_ref[...], preferred_element_type=jnp.float32)
    q_ref[...] = (acc + b_ref[...].astype(jnp.float32)).astype(jnp.bfloat16)


def product_kernel(x_ref, w_ref, b_ref, o_ref):
    acc = jnp.dot(x_ref[...], w_ref[...], preferred_element_type=jnp.float32)
    o_ref[...] = (acc + b_ref[...].astype(jnp.float32)).astype(jnp.bfloat16)


def project_query(pos, own, others, w_query, q_bias, tile):
    rows, width = own.shape
    span = rows * LINE
    cols = w_query.shape[1]
    return pl.pallas_call(
        query_kernel,
        grid_spec=pltpu.PrefetchScalarGridSpec(
            num_scalar_prefetch=1,
            grid=(cols // tile,),
            in_specs=[whole((rows, width))] * (1 + len(others))
            + [pl.BlockSpec((width, tile), lambda i, pos: (0, i)), pl.BlockSpec((1, tile), lambda i, pos: (0, i))],
            out_specs=[pl.BlockSpec((span, tile), lambda i, pos: (0, i)), whole((span, width))],
        ),
        out_shape=[jax.ShapeDtypeStruct((span, cols), jnp.bfloat16), jax.ShapeDtypeStruct((span, width), jnp.bfloat16)],
        compiler_params=params(48, 1),
        name="project_query",
        cost_estimate=pl.CostEstimate(flops=2 * span * width * cols, bytes_accessed=2 * width * cols, transcendentals=0),
    )(pos, own, *others, w_query, q_bias.reshape(1, cols))


def project_fresh(features, w_kv, kv_bias):
    span, width = features.shape
    cols = w_kv.shape[2]
    spec = lambda shape: pl.BlockSpec((None,) + shape, lambda i: (i, 0, 0))
    return pl.pallas_call(
        product_kernel,
        grid=(2,),
        in_specs=[whole((span, width)), spec((width, cols)), spec((1, cols))],
        out_specs=spec((span, cols)),
        out_shape=jax.ShapeDtypeStruct((2, span, cols), jnp.bfloat16),
        compiler_params=params(24, 1),
        name="project_fresh",
        cost_estimate=pl.CostEstimate(flops=4 * span * width * cols, bytes_accessed=4 * width * cols, transcendentals=0),
    )(features, w_kv, kv_bias.reshape(2, 1, cols))


def split2(value):
    high = value.astype(jnp.bfloat16)
    low = (value - high.astype(jnp.float32)).astype(jnp.bfloat16)
    return high, low


def score(q, k):
    dims = (((1,), (1,)), ((), ()))
    return lax.dot_general(q, k, dims, preferred_element_type=jnp.float32) * LOG2E_SCALE


def stack_heads(q_ref, first, count):
    return jnp.concatenate([q_ref[:, (first + i) * HD : (first + i + 1) * HD] for i in range(count)], axis=0)


def put_column(ref, head, column):
    lane = lax.broadcasted_iota(jnp.int32, ref.shape, 1)
    ref[...] = jnp.where(lane == head, column, ref[...])


def shift_of(largest):
    high, low = split2(largest)
    return high.astype(jnp.float32) + low.astype(jnp.float32)


def pack_stats(m, l, heads):
    pieces = [*split2(m[:, :heads]), *split2(l[:, :heads])]
    pad = STAT - 4 * heads
    if pad:
        pieces.append(jnp.zeros((m.shape[0], pad), jnp.bfloat16))
    return jnp.concatenate(pieces, axis=1)


def read_stats(stat, heads):
    stat = stat.astype(jnp.float32)
    m = stat[:, :heads] + stat[:, heads : 2 * heads]
    l = stat[:, 2 * heads : 3 * heads] + stat[:, 3 * heads : 4 * heads]
    return jnp.where(l > 0.0, m, MASKED_SCORE), l


PAIR = 2


def owner_of(kind, z):
    if kind == "up":
        return jnp.maximum(z - 1, 0), z > 0
    if kind == "down":
        return jnp.minimum(z + 1, LINE - 1), z < LINE - 1
    if kind == "two":
        return two_away(z), z >= 0
    return jnp.where(at_end(z), LINE - 1 - z, z), at_end(z)


def far_kernel(kv_here, seq, kinds, info_ref, *refs):
    n_q = len(kinds)
    q_refs, (k_ref, v_ref), out_refs = refs[:n_q], refs[n_q : n_q + 2], refs[n_q + 2 : 2 * n_q + 2]
    m_ref, l_ref = refs[2 * n_q + 2 :]
    way, a = pl.program_id(0), pl.program_id(1)
    z, count = info_ref[0], info_ref[1 + seq]
    heads = kv_here * GROUP
    slots = k_ref.shape[2]
    rows = q_refs[0].shape[0]
    cols = GROUP * HD

    @pl.when(a == 0)
    def _():
        m_ref[...] = jnp.full(m_ref.shape, MASKED_SCORE, jnp.float32)
        l_ref[...] = jnp.zeros(l_ref.shape, jnp.float32)

    def run(q_ref, out_ref, valid):
        live = jnp.logical_and(valid, count > 0)
        for kv in range(kv_here):

            @pl.when(jnp.logical_and(a == kv, live))
            def _():
                keys, values = k_ref[0, 0], v_ref[0, 0]
                slot = lax.broadcasted_iota(jnp.int32, (1, slots), 1)
                bias = jnp.where(slot < count, 0.0, MASKED_SCORE)
                first = score(stack_heads(q_ref, kv * GROUP, PAIR), keys)
                got = []
                for g in range(0, GROUP, PAIR):
                    head = kv * GROUP + g
                    s = first + bias
                    if g + PAIR < GROUP:
                        first = score(stack_heads(q_ref, head + PAIR, PAIR), keys)
                    m = shift_of(jnp.max(s, axis=-1, keepdims=True))
                    p = jnp.exp2(s - m)
                    l = jnp.sum(p, axis=-1, keepdims=True)
                    o = jnp.dot(p.astype(jnp.bfloat16), values, preferred_element_type=jnp.float32)
                    got.append((head, m, l))
                    for i in range(PAIR):
                        part = slice(i * rows, (i + 1) * rows)
                        out_ref[:, (head + i) * HD : (head + i + 1) * HD] = o[part].astype(jnp.bfloat16)
                for head, m, l in got:
                    for i in range(PAIR):
                        part = slice(i * rows, (i + 1) * rows)
                        put_column(m_ref, head + i, m[part])
                        put_column(l_ref, head + i, l[part])

            @pl.when(jnp.logical_and(a == kv, jnp.logical_not(live)))
            def _():
                out_ref[:, kv * cols : (kv + 1) * cols] = jnp.zeros((rows, cols), jnp.bfloat16)

        @pl.when(a == kv_here - 1)
        def _():
            out_ref[:, kv_here * cols :] = pack_stats(m_ref[...], l_ref[...], heads)

    for w, kind in enumerate(kinds):
        pl.when(way == w)(functools.partial(run, q_refs[w], out_refs[w], owner_of(kind, z)[1]))


def attend_far(info, seq, kinds, queries, kv_cache):
    rows, q_cols = queries[0].shape
    slots = kv_cache.shape[2]
    kv_here = q_cols // (GROUP * HD)

    def owner(w, z):
        places = [owner_of(kind, z)[0] for kind in kinds]
        return functools.reduce(lambda rest, i: jnp.where(w == i, places[i], rest), range(len(kinds)), places[0])

    head_at = lambda part: (lambda w, a, info: (seq, part, 0, owner(w, info[0]) * kv_here + a))
    out = jax.ShapeDtypeStruct((rows, q_cols + STAT), jnp.bfloat16)
    return pl.pallas_call(
        functools.partial(far_kernel, kv_here, seq, kinds),
        grid_spec=pltpu.PrefetchScalarGridSpec(
            num_scalar_prefetch=1,
            grid=(len(kinds), kv_here),
            in_specs=[whole((rows, q_cols))] * len(kinds)
            + [pl.BlockSpec((1, 1, slots, HD), head_at(0)), pl.BlockSpec((1, 1, slots, HD), head_at(1))],
            out_specs=[whole((rows, q_cols + STAT))] * len(kinds),
            scratch_shapes=[pltpu.VMEM((rows, 128), jnp.float32), pltpu.VMEM((rows, 128), jnp.float32)],
        ),
        out_shape=[out] * len(kinds),
        compiler_params=params(40, 2),
        name="attend_far",
        cost_estimate=pl.CostEstimate(
            flops=4 * rows * q_cols * slots * len(kinds),
            bytes_accessed=4 * slots * HD * kv_here * len(kinds),
            transcendentals=rows * slots * 8 * len(kinds),
        ),
    )(info, *queries, kv_cache, kv_cache)


def near_kernel(kv_here, seq, info_ref, q_in_ref, k_ref, v_ref, new_ref, o_ref, m_ref, l_ref):
    a = pl.program_id(0)
    count = info_ref[1 + seq]
    heads = kv_here * GROUP
    slots = k_ref.shape[2]
    rows = q_in_ref.shape[0]
    cols = GROUP * HD

    @pl.when(a == 0)
    def _():
        m_ref[...] = jnp.full(m_ref.shape, MASKED_SCORE, jnp.float32)
        l_ref[...] = jnp.zeros(l_ref.shape, jnp.float32)

    for kv in range(kv_here):

        @pl.when(a == kv)
        def _():
            keys, values = k_ref[0, 0], v_ref[0, 0]
            new_keys = new_ref[0, :, kv * HD : (kv + 1) * HD]
            new_values = new_ref[1, :, kv * HD : (kv + 1) * HD]
            slot = lax.broadcasted_iota(jnp.int32, (1, slots), 1)
            bias = jnp.where(slot < count, 0.0, MASKED_SCORE)
            shape = (PAIR * rows, rows)
            token = lax.broadcasted_iota(jnp.int32, shape, 0) % rows
            seen = lax.broadcasted_iota(jnp.int32, shape, 1) <= token
            def scores(head):
                q = stack_heads(q_in_ref, head, PAIR)
                return score(q, keys), score(q, new_keys)

            first = scores(kv * GROUP)
            got = []
            for g in range(0, GROUP, PAIR):
                head = kv * GROUP + g
                s, t = first[0] + bias, jnp.where(seen, first[1], MASKED_SCORE)
                if g + PAIR < GROUP:
                    first = scores(head + PAIR)
                m = jnp.maximum(jnp.max(s, axis=-1, keepdims=True), jnp.max(t, axis=-1, keepdims=True))
                m = shift_of(m)
                p, r = jnp.exp2(s - m), jnp.exp2(t - m)
                l = jnp.sum(p, axis=-1, keepdims=True) + jnp.sum(r, axis=-1, keepdims=True)
                o = jnp.dot(p.astype(jnp.bfloat16), values, preferred_element_type=jnp.float32)
                o += jnp.dot(r.astype(jnp.bfloat16), new_values, preferred_element_type=jnp.float32)
                got.append((head, m, l))
                for i in range(PAIR):
                    part = slice(i * rows, (i + 1) * rows)
                    o_ref[:, (head + i) * HD : (head + i + 1) * HD] = o[part].astype(jnp.bfloat16)
            for head, m, l in got:
                for i in range(PAIR):
                    part = slice(i * rows, (i + 1) * rows)
                    put_column(m_ref, head + i, m[part])
                    put_column(l_ref, head + i, l[part])

    @pl.when(a == kv_here - 1)
    def _():
        o_ref[:, kv_here * cols :] = pack_stats(m_ref[...], l_ref[...], heads)


def attend_near(info, seq, q, fresh, kv_cache):
    rows, q_cols = q.shape
    slots = kv_cache.shape[2]
    kv_here = q_cols // (GROUP * HD)
    head_at = lambda part: (lambda a, info: (seq, part, 0, info[0] * kv_here + a))
    return pl.pallas_call(
        functools.partial(near_kernel, kv_here, seq),
        grid_spec=pltpu.PrefetchScalarGridSpec(
            num_scalar_prefetch=1,
            grid=(kv_here,),
            in_specs=[
                whole((rows, q_cols)),
                pl.BlockSpec((1, 1, slots, HD), head_at(0)),
                pl.BlockSpec((1, 1, slots, HD), head_at(1)),
                whole(fresh.shape),
            ],
            out_specs=whole((rows, q_cols + STAT)),
            scratch_shapes=[pltpu.VMEM((rows, 128), jnp.float32), pltpu.VMEM((rows, 128), jnp.float32)],
        ),
        out_shape=jax.ShapeDtypeStruct((rows, q_cols + STAT), jnp.bfloat16),
        compiler_params=params(40, 1),
        name="attend_near",
        cost_estimate=pl.CostEstimate(
            flops=4 * rows * q_cols * (slots + rows),
            bytes_accessed=4 * slots * HD * kv_here,
            transcendentals=rows * (slots + rows) * 8,
        ),
    )(info, q, kv_cache, kv_cache, fresh)


def join(parts, heads):
    stats = [read_stats(part[:, heads * HD :], heads) for part in parts]
    top = functools.reduce(jnp.maximum, [m for m, _ in stats])
    gains = [jnp.exp2(m - top) for m, _ in stats]
    total = functools.reduce(jnp.add, [g * l for g, (_, l) in zip(gains, stats)])
    return gains, top, total


def joined_head(parts, gains, h):
    cols = slice(h * HD, (h + 1) * HD)
    return functools.reduce(jnp.add, [p[:, cols].astype(jnp.float32) * g[:, h : h + 1] for p, g in zip(parts, gains)])


def join_kernel(heads, a_ref, b_ref, o_ref):
    parts = (a_ref, b_ref)
    gains, top, total = join(parts, heads)
    top = shift_of(top)
    for h in range(heads):
        o_ref[:, h * HD : (h + 1) * HD] = joined_head(parts, gains, h).astype(jnp.bfloat16)
    o_ref[:, heads * HD :] = pack_stats(top, total, heads)


def join_two(a, b):
    rows, width = a.shape
    return pl.pallas_call(
        functools.partial(join_kernel, (width - STAT) // HD),
        out_shape=jax.ShapeDtypeStruct((rows, width), jnp.bfloat16),
        compiler_params=params(24),
        name="join",
        cost_estimate=pl.CostEstimate(flops=8 * a.size, bytes_accessed=6 * a.size, transcendentals=0),
    )(a, b)


def join_pair_kernel(heads, info_ref, a_ref, b_ref, below_ref, above_ref, down_ref, up_ref):
    def run(from_below, from_above):
        for parts, out_ref in (((below_ref, from_above), down_ref), ((above_ref, from_below), up_ref)):
            gains, top, total = join(parts, heads)
            top = shift_of(top)
            for h in range(heads):
                out_ref[:, h * HD : (h + 1) * HD] = joined_head(parts, gains, h).astype(jnp.bfloat16)
            out_ref[:, heads * HD :] = pack_stats(top, total, heads)

    pl.when(info_ref[0] <= 1)(lambda: run(a_ref, b_ref))
    pl.when(info_ref[0] > 1)(lambda: run(b_ref, a_ref))


def join_pair(info, inward, middle, below, above):
    rows, width = below.shape
    out = jax.ShapeDtypeStruct((rows, width), jnp.bfloat16)
    return pl.pallas_call(
        functools.partial(join_pair_kernel, (width - STAT) // HD),
        grid_spec=pltpu.PrefetchScalarGridSpec(
            num_scalar_prefetch=1,
            grid=(1,),
            in_specs=[whole((rows, width))] * 4,
            out_specs=[whole((rows, width))] * 2,
        ),
        out_shape=[out, out],
        compiler_params=params(24, 1),
        name="join_pair",
        cost_estimate=pl.CostEstimate(flops=16 * below.size, bytes_accessed=12 * below.size, transcendentals=0),
    )(info, inward, middle, below, above)


def out_kernel(heads, n_parts, *refs):
    parts, (w_ref, o_ref, x_ref) = refs[:n_parts], refs[n_parts:]

    @pl.when(pl.program_id(0) == 0)
    def _():
        gains, _, total = join(parts, heads)
        inv = 1.0 / total
        gains = [g * inv for g in gains]
        for h in range(heads):
            x_ref[:, h * HD : (h + 1) * HD] = joined_head(parts, gains, h).astype(jnp.bfloat16)

    o_ref[...] = jnp.dot(x_ref[...], w_ref[...], preferred_element_type=jnp.float32).astype(jnp.bfloat16)


def project_out(parts, w_out, tile):
    rows, width = parts[0].shape
    heads = (width - STAT) // HD
    depth, cols = w_out.shape
    return pl.pallas_call(
        functools.partial(out_kernel, heads, len(parts)),
        grid=(cols // tile,),
        in_specs=[whole((rows, width))] * len(parts) + [pl.BlockSpec((depth, tile), lambda i: (0, i))],
        out_specs=pl.BlockSpec((rows, tile), lambda i: (0, i)),
        scratch_shapes=[pltpu.VMEM((rows, depth), jnp.bfloat16)],
        out_shape=jax.ShapeDtypeStruct((rows, cols), jnp.bfloat16),
        compiler_params=params(40, 1),
        name="project_out",
        cost_estimate=pl.CostEstimate(
            flops=2 * rows * depth * cols, bytes_accessed=2 * depth * cols + 2 * rows * cols, transcendentals=0
        ),
    )(*parts, w_out)


UP = [(0, 1), (1, 2), (2, 3)]
DOWN = [(1, 0), (2, 1), (3, 2)]
TWO = [(0, 2), (1, 3), (2, 0), (3, 1)]
MIDDLE = [(1, 2), (2, 1)]
OUTWARD = [(2, 3), (1, 0)]
INWARD = [(0, 1), (3, 2)]


def send(value, pairs):
    return lax.ppermute(value, "tensor", pairs)


def after(value, *earlier):
    return lax.optimization_barrier((value, earlier))[0]


def spread_near(value):
    return send(value, UP), send(value, DOWN), send(value, TWO)


def line_body(residual, norm_gain, scale_exp, w_query, q_bias, w_kv, kv_bias, w_out, kv_cache, offsets):
    z = lax.axis_index("tensor")
    rows = residual.shape[1]
    slots = kv_cache.shape[2]
    counts = jnp.clip(offsets - z * slots, 0, slots)
    info = jnp.concatenate([z.reshape(1), counts]).astype(jnp.int32)
    own0, own1 = encode_tokens(residual, norm_gain, scale_exp)
    tile = 2 * w_kv.shape[2]

    def far(seq, kinds, queries, *earlier):
        queries = list(queries)
        if earlier:
            queries[0] = after(queries[0], *earlier)
        return attend_far(info, seq, kinds, queries, kv_cache)

    def mine(partial, block):
        return lax.dynamic_slice_in_dim(partial, jnp.clip(block, 0, LINE - 1) * rows, rows, axis=0)

    def add(*terms):
        return functools.reduce(jnp.add, [t.astype(jnp.float32) for t in terms]).astype(jnp.bfloat16)

    def neighbours(value, *earlier):
        if earlier:
            value = after(value, *earlier)
        return [send(value, UP), send(value, DOWN)]

    def forward(up, down):
        up, down = send(up, UP[1:]), send(down, DOWN[:2])
        return jnp.where(z >= 2, up, down)

    x0 = neighbours(own0)
    x0.append(forward(*x0))
    x1 = neighbours(own1, x0[2])
    x0.append(send(x0[2], OUTWARD))
    q0, x0_all = project_query(info, after(own0, *x1), x0, w_query, q_bias, tile)
    x1.append(forward(*x1))
    x1.append(send(x1[2], OUTWARD))
    g0 = neighbours(q0)
    fresh0 = project_fresh(x0_all, w_kv, kv_bias)
    near0 = attend_near(info, 0, q0, fresh0, kv_cache)
    g0.append(forward(after(g0[0], near0), after(g0[1], near0)))
    q1, x1_all = project_query(info, after(own1, near0, g0[0]), x1, w_query, q_bias, tile)
    g0.append(send(after(g0[2], q1), OUTWARD))
    g1 = neighbours(q1)
    below0, above0 = far(0, ("up", "down"), g0[:2], q1)
    g1.append(forward(after(g1[0], below0), after(g1[1], below0)))
    (two0,) = far(0, ("two",), g0[2:3], below0)
    (three0,) = far(0, ("three",), g0[3:], two0)
    h0_three = send(three0, INWARD)
    g1.append(send(after(g1[2], two0), OUTWARD))
    fresh1 = project_fresh(after(x1_all, three0), w_kv, kv_bias)
    near1 = attend_near(info, 1, q1, fresh1, kv_cache)
    joined0 = join_two(after(h0_three, near1), two0)
    h0_inward, h0_middle = send(joined0, INWARD), send(joined0, MIDDLE)
    below1, above1 = far(1, ("up", "down"), g1[:2], joined0)
    (two1,) = far(1, ("two",), g1[2:3], below1)
    (three1,) = far(1, ("three",), g1[3:], two1)
    h1_three = send(three1, INWARD)
    down0, up0 = join_pair(info, after(h0_inward, three1), h0_middle, below0, above0)
    h0_down, h0_up = send(down0, DOWN), send(up0, UP)
    joined1 = join_two(after(h1_three, down0), two1)
    h1_inward, h1_middle = send(joined1, INWARD), send(joined1, MIDDLE)
    partial0 = project_out([near0, h0_up, after(h0_down, joined1)], w_out, 2048)
    down1, up1 = join_pair(info, after(h1_inward, partial0), h1_middle, below1, above1)
    h1_down, h1_up = send(down1, DOWN), send(up1, UP)

    def one_home(partial, inward):
        joined = add(inward, mine(partial, two_away(z)))
        return send(joined, INWARD), send(joined, MIDDLE)

    def two_home(partial, inward, middle):
        up = add(mine(partial, z + 1), jnp.where(z <= 1, inward, middle))
        down = add(mine(partial, z - 1), jnp.where(z <= 1, middle, inward))
        return send(up, UP), send(down, DOWN)

    s0 = send(mine(partial0, LINE - 1 - z), INWARD)
    partial1 = project_out([near1, h1_up, h1_down], w_out, 2048)
    s1 = send(mine(partial1, LINE - 1 - z), INWARD)
    s0, s1 = one_home(partial0, s0), one_home(partial1, s1)
    s0, s1 = two_home(partial0, *s0), two_home(partial1, *s1)
    mixed0 = add(mine(partial0, z), *s0)
    mixed1 = add(mine(partial1, z), *s1)
    fresh = after(jnp.stack([fresh0, fresh1]), partial1)
    new_kv = lax.all_to_all(fresh, "tensor", split_axis=2, concat_axis=3, tiled=True)
    return jnp.stack([mixed0, mixed1]), new_kv


def body(*args):
    heads_here = args[3].shape[1] // HD
    tensor_size = lax.axis_size("tensor")
    if heads_here % GROUP == 0 and args[0].shape[0] == 2 and tensor_size == LINE:
        return line_body(*args)
    return general_body(*args)


def solution(mesh):
    placed = (
        P(("groups", "dp"), "tensor", None),
        P(),
        P(("groups", "dp"), "tensor", None),
        P(None, "tensor"),
        P("tensor"),
        P(None, None, "tensor"),
        P(None, "tensor"),
        P("tensor", None),
        P(("groups", "dp"), None, "tensor", None),
        P(("groups", "dp")),
    )
    return jax.shard_map(
        body,
        mesh=mesh,
        in_specs=placed,
        out_specs=(P(("groups", "dp"), "tensor", None), P(("groups", "dp"), None, "tensor", None)),
        check_vma=False,
    )
```
